32 devices in a mesh: cls: 2 (over core), ptcl: 16 (over z, y, x).
Axes of the slice: x: 2, y: 2, z: 4, core: 2. Of those that a mesh axis runs over, the one named last changes fastest.
Arguments:
- particles: bfloat16 [16384, 2048], P('ptcl')
- panels: bfloat16 [2, 128, 2048], P('cls', 'ptcl')
- sigma2: float32 [32], replicated, may hold values from 0.5 to 2
- defocus_bins: int32 [16384], P('ptcl'), may hold values from 0 to 15
- half_sets: int32 [16384], P('ptcl'), may hold values 0 or 1
- prior_mask: int32 [16384, 2], P('ptcl', 'cls'), may hold values from 0 to 1, as said below
- orient_ids: int32 [128], replicated, may hold values from 0 to 127, each once
Outputs:
- half_maps: float32 [2, 256, 2048], P('cls', 'ptcl')
- log_evidence: float32 [16384], P('ptcl')
The draws below stay inside these ranges and needn't reach their ends.
Inputs may be any that keep to these rules, and one draw needn't show every extreme that they name: `prior_mask`: every particle allows at least one class. `orient_ids`: each direction 0 to 127 appears once.
All inputs are finite; a program needn't handle non-finite values. No bound on the sum of `half_sets` on one device may be relied on, other than what follows from the above.
Results may differ from the reference program's by a relative error of at most 0.0015.
The reference program's roundings to bfloat16 on the way (of `weighted`, `power`, `panel_power`, `by_direction` and `centred`) count: a program that leaves them out, or rounds other values in their place, can miss the bound.
Values may be sent and summed in bfloat16 or wider, within the bound.
A program may use at most 64 MiB of HBM per device.

```python
import math
import jax
import jax.numpy as jnp
from jax import lax

PIXC = 1024
ORIENT = 128
NSHELL = 32
NBIN = 16
PTCLS = 16384
CLASSES = 2


def ctf_values(bins):
    defocus = (bins.astype(jnp.float32) + 1.0) / NBIN
    radius = (jnp.arange(PIXC, dtype=jnp.float32) + 0.5) / PIXC
    phase = 0.3 + 2.5 * defocus[:, None] * radius[None, :]
    return jnp.sin(phase) + 0.1 * jnp.cos(phase)


def source_labels(key):
    classes = jax.random.randint(jax.random.fold_in(key, 101), (PTCLS,), 0, CLASSES)
    orients = jax.random.randint(jax.random.fold_in(key, 102), (PTCLS,), 0, ORIENT)
    bins = jax.random.randint(jax.random.fold_in(key, 103), (PTCLS,), 0, NBIN)
    return (classes, orients, bins)


def panel_values(key):
    shape = (CLASSES, ORIENT, 2 * PIXC)
    spread = 3.0 / PIXC ** 0.5
    values = spread * jax.random.normal(jax.random.fold_in(key, 201), shape, jnp.float32)
    near = values[:, 0] + 0.03 * spread * jax.random.normal(jax.random.fold_in(key, 202), (CLASSES, 2 * PIXC), jnp.float32)
    values = values.at[:, 1].set(near)
    return values


def draw_panels(key, part):
    return panel_values(key).astype(jnp.bfloat16)


def draw_defocus_bins(key, part):
    return source_labels(key)[2].astype(jnp.int32)


def draw_prior_mask(key, part):
    classes = source_labels(key)[0]
    coin = jax.random.randint(jax.random.fold_in(key, 301), (PTCLS, CLASSES), 0, 2)
    own = (classes[:, None] == jnp.arange(CLASSES)[None, :]).astype(jnp.int32)
    return jnp.maximum(coin, own).astype(jnp.int32)


def draw_particles(key, part):
    classes, orients, bins = source_labels(key)
    rows = jnp.arange(PTCLS)
    strong = rows % 97 == 0
    amplitude = jnp.where(strong, 16.0 + 8.0 * (rows // 97 % 3).astype(jnp.float32), 1.0)
    orients = jnp.where(strong, 0, orients)
    signal = panel_values(key)[classes, orients]
    contrast = ctf_values(bins)
    doubled = jnp.concatenate([contrast, contrast], axis=1)
    noise = jax.random.normal(jax.random.fold_in(key, 401), (PTCLS, 2 * PIXC), jnp.float32)
    return (amplitude[:, None] * doubled * signal + noise).astype(jnp.bfloat16)


def plant(result, own_key, least, high):
    index_at = [jax.random.randint(jax.random.fold_in(own_key, axis), (), 0, length) for axis, length in enumerate(result.shape)]
    widest = result.shape.index(max(result.shape))
    beside = index_at[:widest] + [(index_at[widest] + 1) % result.shape[widest]] + index_at[widest + 1:]
    return result.at[tuple(index_at)].set(least).at[tuple(beside)].set(high)


def setup_inputs(seed: int = 0) -> dict:
    key_list = jax.random.split(jax.random.key(seed), 8)
    return {
        "particles": draw_particles(jax.random.fold_in(key_list[7], 71), 0),
        "panels": draw_panels(jax.random.fold_in(key_list[7], 71), 0),
        "sigma2": jnp.clip(jnp.exp(jax.random.uniform(key_list[2], (NSHELL,), jnp.float32, math.log(0.5), math.log(2.0))), 0.5, 2.0),
        "defocus_bins": draw_defocus_bins(jax.random.fold_in(key_list[7], 71), 0),
        "half_sets": plant((jax.random.randint(key_list[4], (PTCLS,), 0, 2) < 1).astype(jnp.int32), jax.random.fold_in(key_list[4], 1), 0, 1),
        "prior_mask": draw_prior_mask(jax.random.fold_in(key_list[7], 71), 0),
        "orient_ids": jax.random.permutation(key_list[6], ORIENT).astype(jnp.int32),
    }


def ctf_table():
    bins = jnp.arange(NBIN, dtype=jnp.float32)
    defocus = (bins + 1.0) / NBIN
    radius = (jnp.arange(PIXC, dtype=jnp.float32) + 0.5) / PIXC
    phase = 0.3 + 2.5 * defocus[:, None] * radius[None, :]
    return jnp.sin(phase) + 0.1 * jnp.cos(phase)

def reference(particles, panels, sigma2, defocus_bins, half_sets, prior_mask, orient_ids):
    shells = jnp.arange(PIXC, dtype=jnp.int32) * NSHELL // PIXC
    inverse_noise = 1.0 / sigma2[shells]
    contrast = ctf_table()[defocus_bins]
    doubled = jnp.concatenate([contrast, contrast], axis=1)
    noise_pair = jnp.concatenate([inverse_noise, inverse_noise])
    images = particles.astype(jnp.float32)
    weighted = (images * doubled * noise_pair[None, :]).astype(jnp.bfloat16)
    power = (contrast * contrast * inverse_noise[None, :]).astype(jnp.bfloat16)
    panel_f = panels.astype(jnp.float32)
    panel_power = (panel_f[..., :PIXC] ** 2 + panel_f[..., PIXC:] ** 2).astype(jnp.bfloat16)
    flat_panels = panels.reshape(CLASSES * ORIENT, 2 * PIXC)
    flat_power = panel_power.reshape(CLASSES * ORIENT, PIXC)
    scores = jnp.dot(weighted, flat_panels.T, preferred_element_type=jnp.float32)
    scores = scores - 0.5 * jnp.dot(power, flat_power.T, preferred_element_type=jnp.float32)
    scores = scores.reshape(PTCLS, CLASSES, ORIENT)
    allowed = (prior_mask > 0)[:, :, None]
    masked = jnp.where(allowed, scores, -1e+30)
    peak = lax.optimization_barrier(jnp.max(masked, axis=(1, 2)))
    weights_exp = jnp.where(allowed, jnp.exp(masked - peak[:, None, None]), 0.0)
    total = lax.optimization_barrier(jnp.sum(weights_exp, axis=(1, 2)))
    log_evidence = peak + jnp.log(total)
    posterior = (weights_exp / total[:, None, None]).astype(jnp.bfloat16)
    inverse = jnp.zeros((ORIENT,), jnp.int32).at[orient_ids].set(jnp.arange(ORIENT, dtype=jnp.int32))
    by_direction = posterior[:, :, inverse]
    half_col = half_sets.astype(jnp.bfloat16)[:, None, None]
    split_post = jnp.stack([by_direction * (1 - half_col), by_direction * half_col], axis=2)
    flat_post = split_post.reshape(PTCLS, CLASSES * 2 * ORIENT)
    centred = (images * doubled).astype(jnp.bfloat16)
    squares_ctf = (contrast * contrast).astype(jnp.bfloat16)
    data = jnp.dot(flat_post.T, centred, preferred_element_type=jnp.float32).reshape(CLASSES, 2, ORIENT, 2 * PIXC)
    weight = jnp.dot(flat_post.T, squares_ctf, preferred_element_type=jnp.float32).reshape(CLASSES, 2, ORIENT, PIXC)

    def per_shell(values):
        summed = lax.optimization_barrier(jnp.sum(values, axis=1))
        folded = summed[:, :PIXC] + summed[:, PIXC:]
        return lax.optimization_barrier(jnp.sum(folded.reshape(CLASSES, NSHELL, PIXC // NSHELL), axis=2))
    cross = per_shell(data[:, 0] * data[:, 1])
    power_zero = per_shell(data[:, 0] * data[:, 0])
    power_one = per_shell(data[:, 1] * data[:, 1])
    fsc = cross / jnp.sqrt(power_zero * power_one + 1e-06)
    factor = (1.0 + fsc[:, shells]) / 2.0
    factor_pair = jnp.concatenate([factor, factor], axis=1)
    weight_pair = jnp.concatenate([weight, weight], axis=3)
    half_maps = data * factor_pair[:, None, None, :] / (weight_pair + 1.0)
    return (half_maps.reshape(CLASSES, 2 * ORIENT, 2 * PIXC), log_evidence)
```

```python
import functools

import jax
import jax.numpy as jnp
import numpy as np
from jax import lax
from jax.experimental import pallas as pl
from jax.experimental.pallas import tpu as pltpu
from jax.sharding import PartitionSpec as P

PIXC = 1024
ORIENT = 128
NSHELL = 32
NBIN = 16
LANES = 128
WIDTH = 2 * PIXC + LANES
CHUNKS = ((1536, 640), (0, 512), (512, 512), (1024, 512))
MESH = pl.DeviceIdType.MESH
BF16 = jnp.bfloat16
F32 = jnp.float32


def ctf_table():
    defocus = (np.arange(NBIN, dtype=np.float32) + np.float32(1.0)) / np.float32(NBIN)
    radius = (np.arange(PIXC, dtype=np.float32) + np.float32(0.5)) / np.float32(PIXC)
    phase = np.float32(0.3) + np.float32(2.5) * defocus[:, None] * radius[None, :]
    wide = phase.astype(np.float64)
    return (np.sin(wide) + 0.1 * np.cos(wide)).astype(np.float32)


def iota(shape, dim):
    return lax.broadcasted_iota(jnp.int32, shape, dim)


def dot(left, right):
    return lax.dot_general(left, right, (((1,), (0,)), ((), ())), preferred_element_type=F32)


def dot_t(left, right):
    return lax.dot_general(left, right, (((1,), (1,)), ((), ())), preferred_element_type=F32)


def split3(values):
    high = values.astype(BF16)
    rest = values - high.astype(F32)
    mid = rest.astype(BF16)
    low = (rest - mid.astype(F32)).astype(BF16)
    return high, mid, low


def exact(values, product):
    high, mid, low = split3(values)
    return product(high) + product(mid) + product(low)


def by_group(values, dim):
    high, mid, low = split3(values)
    group = iota(values.shape, dim) // NBIN
    mixed = jnp.where(
        group == 0,
        high.astype(F32),
        jnp.where(group == 1, mid.astype(F32), jnp.where(group == 2, low.astype(F32), 0.0)),
    )
    return mixed.astype(BF16)


def kernel(
    dims,
    particles,
    panels,
    sigma2,
    bins,
    halves,
    prior,
    orient,
    table,
    maps,
    evidence,
    images,
    weighted,
    centred,
    gathered,
    onehot,
    tables,
    noise,
    peaks,
    posts,
    send1,
    recv1,
    acc,
    recv2,
    final,
    swapped,
    stats,
    load_sem,
    gsend,
    grecv,
    csend,
    crecv,
    s1send,
    s1recv,
    s2send,
    s2recv,
    xsend,
    xrecv,
    tsend,
    trecv,
):
    n, ncls, plane, line, rows, pad, count = dims
    block = 2 * pad
    total_rows = n * block
    own_rows = line * block
    me = lax.axis_index("ptcl")
    mine = lax.axis_index("cls")
    q = lax.rem(me, plane)
    l = me // plane
    half = me // (n // 2)

    def at(line_pos, plane_pos):
        return line_pos * plane + plane_pos

    def remote(src, dst, send, recv, ptcl=None, cls=None):
        return pltpu.make_async_remote_copy(
            src_ref=src,
            dst_ref=dst,
            send_sem=send,
            recv_sem=recv,
            device_id=(mine if cls is None else cls, me if ptcl is None else ptcl),
            device_id_type=MESH,
        )

    barrier = pltpu.get_barrier_semaphore()
    for i in range(1, n):
        pl.semaphore_signal(
            barrier, inc=1, device_id=(mine, lax.rem(me + i, n)), device_id_type=MESH
        )
    for i in range(1, ncls):
        pl.semaphore_signal(
            barrier, inc=1, device_id=(lax.rem(mine + i, ncls), me), device_id_type=MESH
        )
    quarter = count // 4
    loads = []
    for i in range(4):
        span = pl.ds(i * quarter, quarter)
        loads.append(
            pltpu.make_async_copy(particles.at[span], images.at[span], load_sem.at[i])
        )
        loads[-1].start()

    piece = panels[0].astype(F32)
    real, imag = piece[:, :PIXC], piece[:, PIXC:]
    if rows < pad:
        fill = jnp.zeros((pad - rows, PIXC), F32)
        parts = [real, fill, imag, fill]
    else:
        parts = [real, imag]

    def spot(device):
        return gathered.at[pl.ds(pl.multiple_of(device * block, block), block)]

    gathered[pl.ds(pl.multiple_of(me * block, block), block), :] = jnp.concatenate(
        parts, axis=0
    ).astype(BF16)
    pl.semaphore_wait(barrier, n - 1 + ncls - 1)

    sends = []
    line_copies = [None]
    for i in range(1, line):
        copy = remote(
            spot(me), spot(me), gsend.at[i, 0], grecv.at[i, 0], at(lax.rem(l + i, line), q)
        )
        copy.start()
        line_copies.append(copy)
    plane_copies = []

    def forward(i):
        source = at(lax.rem(l + line - i, line), q)
        for p in range(1, plane):
            copy = remote(
                spot(source),
                spot(source),
                gsend.at[i, p],
                grecv.at[i, p],
                at(l, lax.rem(q + p, plane)),
            )
            copy.start()
            plane_copies.append(copy)

    forward(0)

    shell_pick = (iota((LANES, PIXC), 0) == iota((LANES, PIXC), 1) // (PIXC // NSHELL)).astype(
        F32
    ).astype(BF16)
    inverse = jnp.broadcast_to(1.0 / sigma2[...], (8, NSHELL))
    noise[...] = exact(inverse, lambda v: dot(v, shell_pick[:NSHELL]))
    base = table[...]
    base = jnp.concatenate(
        [base, base, base, jnp.zeros((LANES - 3 * NBIN, PIXC), F32)], axis=0
    )
    tables[0] = by_group(base, 0)
    tables[1] = (base * base * noise[0:1, :]).astype(BF16)
    tables[2] = (base * base).astype(BF16)
    row = iota((LANES, count), 0)
    onehot[...] = (
        jnp.where((row < 3 * NBIN) & (lax.rem(row, NBIN) == bins[...]), 1.0, 0.0)
    ).astype(BF16)

    step = LANES

    def prepare(first, last):
        def body(i, carry):
            span = pl.ds(pl.multiple_of(i * step, step), step)
            picks = onehot[:, span]
            contrast = lax.dot_general(
                picks, tables[0], (((0,), (0,)), ((), ())), preferred_element_type=F32
            )
            level = noise[0:1, :]
            for part in range(2):
                cols = slice(part * PIXC, (part + 1) * PIXC)
                product = images[span, cols].astype(F32) * contrast
                centred[span, cols] = product.astype(BF16)
                weighted[span, cols] = (product * level).astype(BF16)
            return carry

        lax.fori_loop(first, last, body, 0)

    per = quarter // step
    for i in range(4):
        loads[i].wait()
        if i == 2:
            for s in range(1, line):
                line_copies[s].wait_recv()
                forward(s)
        prepare(i * per, (i + 1) * per)

    ids = jnp.broadcast_to(orient[...].astype(F32), (8, ORIENT)).astype(BF16)
    shape = (ORIENT, total_rows)
    col = iota(shape, 1)
    within = lax.rem(col, pad)
    expand = jnp.where(
        (col // block * rows + within == iota(shape, 0)) & (within < rows), 1.0, 0.0
    ).astype(BF16)
    ids_cols = dot(ids, expand)[0:1, :]
    square = (total_rows, total_rows)
    r = iota((total_rows, 1), 0)
    slot = lax.rem(r, pad)
    r_line = lax.rem(lax.rem(r // block, line) + l, line)
    r_plane = lax.rem(r // own_rows + q, plane)
    owner = at(r_line, r_plane)
    pairs = n // 2
    direction = lax.rem(owner, pairs) * (2 * rows) + owner // pairs * rows + slot
    direction = jnp.where(slot < rows, direction, -1).astype(F32)
    c = iota((1, total_rows), 1)
    c_part = lax.rem(c // pad, 2)
    c_ok = lax.rem(c, pad) < rows
    real_ids = jnp.where(c_ok & (c_part == 0), ids_cols, -2.0)
    imag_ids = jnp.where(c_ok & (c_part == 1), ids_cols, -2.0)
    pick_real = jnp.where(jnp.broadcast_to(direction, square) == real_ids, 1.0, 0.0).astype(BF16)
    pick_imag = jnp.where(jnp.broadcast_to(direction, square) == imag_ids, 1.0, 0.0).astype(BF16)
    row_half = lax.rem(r // pad, 2)

    for copy in plane_copies:
        copy.wait_recv()
    whole = gathered[...]
    panel_real = dot(pick_real, whole)
    panel_imag = dot(pick_imag, whole)
    panel_power = (panel_real * panel_real + panel_imag * panel_imag).astype(BF16)
    norm = by_group(dot_t(panel_power, tables[1]), 1)
    scores = (
        dot_t(panel_real.astype(BF16), weighted[:, :PIXC])
        + dot_t(panel_imag.astype(BF16), weighted[:, PIXC:])
        - 0.5 * dot(norm, onehot[...])
    )
    use = (prior[...] > 0) & (halves[...] == row_half) & (slot < rows)
    masked = jnp.where(use, scores, -1e30)
    local_peak = jnp.max(masked, axis=0, keepdims=True)
    raw = jnp.where(use, jnp.exp(masked - local_peak), 0.0)
    local_total = jnp.sum(raw, axis=0, keepdims=True)
    peaks[0, 0:1, :] = local_peak
    peaks[0, 1:2, :] = local_total
    class_copies = []
    for i in range(1, ncls):
        copy = remote(
            peaks.at[0],
            peaks.at[i],
            csend.at[i],
            crecv.at[i],
            cls=lax.rem(mine + i, ncls),
        )
        copy.start()
        class_copies.append(copy)
    for copy in class_copies:
        copy.wait_recv()
    peak = local_peak
    for i in range(1, ncls):
        peak = jnp.maximum(peak, peaks[i, 0:1, :])
    total = local_total * jnp.exp(local_peak - peak)
    for i in range(1, ncls):
        total = total + peaks[i, 1:2, :] * jnp.exp(peaks[i, 0:1, :] - peak)
    posts[...] = (raw * (jnp.exp(local_peak - peak) / total)).astype(BF16)
    evidence[...] = peak + jnp.log(total)

    plane_sends = []
    for k, (start, width) in enumerate(CHUNKS):
        data_width = min(width, 2 * PIXC - start)
        part = dot(posts[...], centred[:, start : start + data_width])
        acc[:, start : start + data_width] = part[:own_rows]
        send1[:, start : start + data_width] = part[own_rows:].astype(BF16)
        if data_width < width:
            sums = dot_t(posts[...], onehot[...])
            acc[:, 2 * PIXC :] = jnp.where(
                iota((own_rows, LANES), 1) < NBIN, sums[:own_rows], 0.0
            )
            send1[:, 2 * PIXC :] = by_group(sums[own_rows:], 1)
        cols = pl.ds(start, width)
        group = []
        for p in range(1, plane):
            copy = remote(
                send1.at[pl.ds((p - 1) * own_rows, own_rows), cols],
                recv1.at[p - 1, :, cols],
                s1send.at[k, p],
                s1recv.at[k, p],
                at(l, lax.rem(q + p, plane)),
            )
            copy.start()
            group.append(copy)
        plane_sends.append(group)

    line_sends = []
    for k, (start, width) in enumerate(CHUNKS):
        cols = pl.ds(start, width)
        for copy in plane_sends[k]:
            copy.wait_recv()
        value = acc[:, start : start + width]
        for p in range(1, plane):
            value = value + recv1[p - 1, :, start : start + width].astype(F32)
        acc[:, start : start + width] = value
        group = []
        for i in range(1, line):
            copy = remote(
                acc.at[pl.ds(i * block, block), cols],
                recv2.at[i - 1, :, cols],
                s2send.at[k, i],
                s2recv.at[k, i],
                at(lax.rem(l + i, line), q),
            )
            copy.start()
            group.append(copy)
        line_sends.append(group)

    for k, (start, width) in enumerate(CHUNKS):
        for copy in line_sends[k]:
            copy.wait_recv()
        value = acc[:block, start : start + width]
        for i in range(1, line):
            value = value + recv2[i - 1, :, start : start + width]
        final[0, :, start : start + width] = value[:pad]
        final[1, :, start : start + width] = value[pad:]

    swap = remote(
        final.at[1 - half],
        swapped.at[half],
        xsend,
        xrecv,
        lax.rem(me + n // 2, n),
    )
    swap.start()
    first = final[0, :, : 2 * PIXC]
    second = final[1, :, : 2 * PIXC]

    def folded(values):
        summed = jnp.sum(values, axis=0, keepdims=True)
        return summed[:, :PIXC] + summed[:, PIXC:]

    table_rows = jnp.concatenate(
        [
            folded(first * second),
            folded(first * first),
            folded(second * second),
            jnp.zeros((5, PIXC), F32),
        ],
        axis=0,
    )
    stats[0] = exact(table_rows, lambda v: dot_t(v, shell_pick))
    stat_copies = []
    for i in range(1, n):
        copy = remote(
            stats.at[0], stats.at[i], tsend.at[i], trecv.at[i], lax.rem(me + i, n)
        )
        copy.start()
        stat_copies.append(copy)
    kept = final[half]
    swap.wait_recv()
    swapped[half] = kept
    ready = []
    for h in range(2):
        bin_sums = swapped[h, :, 2 * PIXC :]
        ready.append(1.0 + exact(bin_sums, lambda v: dot(v, tables[2])))
    for copy in stat_copies:
        copy.wait_recv()
    sums = stats[0]
    for i in range(1, n):
        sums = sums + stats[i]
    fsc = sums[0:1] / jnp.sqrt(sums[1:2] * sums[2:3] + 1e-06)
    factor = jnp.broadcast_to((1.0 + fsc) / 2.0, (8, LANES))
    factor = exact(factor, lambda v: dot(v, shell_pick))[0:1, :]
    for h in range(2):
        for part in range(2):
            cols = slice(part * PIXC, (part + 1) * PIXC)
            value = swapped[h, :, cols] * factor / ready[h]
            maps[0, h * rows : (h + 1) * rows, cols] = value[:rows]

    for copy in line_copies[1:] + plane_copies + class_copies + stat_copies + [swap]:
        copy.wait_send()
    for group in plane_sends + line_sends:
        for copy in group:
            copy.wait_send()


def solution(mesh):
    n = mesh.shape["ptcl"]
    ncls = mesh.shape["cls"]
    plane = 4
    line = n // plane
    rows = ORIENT // n
    pad = max(8, rows)
    block = 2 * pad
    own_rows = line * block
    nchunks = len(CHUNKS)

    def on_device(particles, panels, sigma2, defocus_bins, half_sets, prior_mask, orient_ids):
        count = particles.shape[0]
        dims = (n, ncls, plane, line, rows, pad, count)
        vmem = pl.BlockSpec(memory_space=pltpu.VMEM)
        dma = pltpu.SemaphoreType.DMA
        maps, evidence = pl.pallas_call(
            functools.partial(kernel, dims),
            out_shape=(
                jax.ShapeDtypeStruct((1, 2 * rows, 2 * PIXC), F32),
                jax.ShapeDtypeStruct((1, count), F32),
            ),
            in_specs=[pl.BlockSpec(memory_space=pl.ANY)] + [vmem] * 7,
            out_specs=(vmem, vmem),
            scratch_shapes=[
                pltpu.VMEM((count, 2 * PIXC), BF16),
                pltpu.VMEM((count, 2 * PIXC), BF16),
                pltpu.VMEM((count, 2 * PIXC), BF16),
                pltpu.VMEM((n * block, PIXC), BF16),
                pltpu.VMEM((LANES, count), BF16),
                pltpu.VMEM((3, LANES, PIXC), BF16),
                pltpu.VMEM((8, PIXC), F32),
                pltpu.VMEM((ncls, 2, count), F32),
                pltpu.VMEM((n * block, count), BF16),
                pltpu.VMEM((n * block - own_rows, WIDTH), BF16),
                pltpu.VMEM((plane - 1, own_rows, WIDTH), BF16),
                pltpu.VMEM((own_rows, WIDTH), F32),
                pltpu.VMEM((line - 1, block, WIDTH), F32),
                pltpu.VMEM((2, pad, WIDTH), F32),
                pltpu.VMEM((2, pad, WIDTH), F32),
                pltpu.VMEM((n, 8, LANES), F32),
                dma((4,)),
                dma((line, plane)),
                dma((line, plane)),
                dma((ncls,)),
                dma((ncls,)),
                dma((nchunks, plane)),
                dma((nchunks, plane)),
                dma((nchunks, line)),
                dma((nchunks, line)),
                dma,
                dma,
                dma((n,)),
                dma((n,)),
            ],
            compiler_params=pltpu.CompilerParams(
                collective_id=0, has_side_effects=True, vmem_limit_bytes=56 * 2**20
            ),
        )(
            particles,
            panels,
            sigma2.reshape(1, NSHELL),
            defocus_bins.reshape(1, count),
            half_sets.reshape(1, count),
            prior_mask.reshape(1, count),
            orient_ids.reshape(1, ORIENT),
            jnp.asarray(ctf_table()),
        )
        return maps, evidence.reshape(count)

    return jax.shard_map(
        on_device,
        mesh=mesh,
        in_specs=(
            P("ptcl", None),
            P("cls", "ptcl", None),
            P(),
            P("ptcl"),
            P("ptcl"),
            P("ptcl", "cls"),
            P(),
        ),
        out_specs=(P("cls", "ptcl", None), P("ptcl")),
        check_vma=False,
    )
```

```python
import functools

import jax
import jax.numpy as jnp
import numpy as np
from jax import lax
from jax.experimental import pallas as pl
from jax.experimental.pallas import tpu as pltpu
from jax.sharding import PartitionSpec as P

PIXC = 1024
ORIENT = 128
NSHELL = 32
NBIN = 16
LANES = 128
WIDTH = 2 * PIXC + LANES
CHUNK = 256
CHUNKS = ((2 * PIXC - CHUNK, CHUNK + LANES),) + tuple(
    (start, CHUNK) for start in range(0, 2 * PIXC - CHUNK, CHUNK)
)
WINDOW = 3
MESH = pl.DeviceIdType.MESH
BF16 = jnp.bfloat16
F32 = jnp.float32


def ctf_table():
    defocus = (np.arange(NBIN, dtype=np.float32) + np.float32(1.0)) / np.float32(NBIN)
    radius = (np.arange(PIXC, dtype=np.float32) + np.float32(0.5)) / np.float32(PIXC)
    phase = np.float32(0.3) + np.float32(2.5) * defocus[:, None] * radius[None, :]
    wide = phase.astype(np.float64)
    return (np.sin(wide) + 0.1 * np.cos(wide)).astype(np.float32)


def iota(shape, dim):
    return lax.broadcasted_iota(jnp.int32, shape, dim)


def dot(left, right):
    return lax.dot_general(left, right, (((1,), (0,)), ((), ())), preferred_element_type=F32)


def dot_t(left, right):
    return lax.dot_general(left, right, (((1,), (1,)), ((), ())), preferred_element_type=F32)


def split3(values):
    high = values.astype(BF16)
    rest = values - high.astype(F32)
    mid = rest.astype(BF16)
    low = (rest - mid.astype(F32)).astype(BF16)
    return high, mid, low


def exact(values, product):
    high, mid, low = split3(values)
    return product(high) + product(mid) + product(low)


def by_group(values, dim):
    high, mid, low = split3(values)
    group = iota(values.shape, dim) // NBIN
    mixed = jnp.where(
        group == 0,
        high.astype(F32),
        jnp.where(group == 1, mid.astype(F32), jnp.where(group == 2, low.astype(F32), 0.0)),
    )
    return mixed.astype(BF16)


def kernel(
    dims,
    particles,
    panels,
    sigma2,
    bins,
    halves,
    prior,
    orient,
    table,
    maps,
    evidence,
    images,
    weighted,
    centred,
    gathered,
    onehot,
    tables,
    noise,
    peaks,
    posts,
    send1,
    recv1,
    acc,
    recv2,
    recv3,
    final,
    swapped,
    shells,
    stats,
    load_sem,
    gsend,
    grecv,
    csend,
    crecv,
    s1send,
    s1recv,
    s2send,
    s2recv,
    xsend,
    xrecv,
    tsend,
    trecv,
):
    n, ncls, plane, line, rows, pad, count = dims
    block = 2 * pad
    total_rows = n * block
    own_rows = line * block
    pair_rows = own_rows // 2
    me = lax.axis_index("ptcl")
    mine = lax.axis_index("cls")
    q = lax.rem(me, plane)
    l = me // plane
    half = me // (n // 2)

    pair = l // 2
    kind = lax.rem(l + pair, 2)

    def line_of(pair_pos, wanted):
        return 2 * pair_pos + lax.rem(pair_pos + wanted, 2)

    def at(line_pos, plane_pos):
        return line_pos * plane + plane_pos

    def remote(src, dst, send, recv, ptcl=None, cls=None):
        return pltpu.make_async_remote_copy(
            src_ref=src,
            dst_ref=dst,
            send_sem=send,
            recv_sem=recv,
            device_id=(mine if cls is None else cls, me if ptcl is None else ptcl),
            device_id_type=MESH,
        )

    barrier = pltpu.get_barrier_semaphore()
    for i in range(1, n):
        pl.semaphore_signal(
            barrier, inc=1, device_id=(mine, lax.rem(me + i, n)), device_id_type=MESH
        )
    for i in range(1, ncls):
        pl.semaphore_signal(
            barrier, inc=1, device_id=(lax.rem(mine + i, ncls), me), device_id_type=MESH
        )
    quarter = count // 4
    loads = []
    for i in range(4):
        span = pl.ds(i * quarter, quarter)
        loads.append(
            pltpu.make_async_copy(particles.at[span], images.at[span], load_sem.at[i])
        )
        loads[-1].start()

    piece = panels[0].astype(F32)
    real, imag = piece[:, :PIXC], piece[:, PIXC:]
    if rows < pad:
        fill = jnp.zeros((pad - rows, PIXC), F32)
        parts = [real, fill, imag, fill]
    else:
        parts = [real, imag]

    def spot(device):
        return gathered.at[pl.ds(pl.multiple_of(device * block, block), block)]

    gathered[pl.ds(pl.multiple_of(me * block, block), block), :] = jnp.concatenate(
        parts, axis=0
    ).astype(BF16)
    pl.semaphore_wait(barrier, n - 1 + ncls - 1)

    sends = []
    line_copies = [None]
    for i in range(1, line):
        copy = remote(
            spot(me), spot(me), gsend.at[i, 0], grecv.at[i, 0], at(lax.rem(l + i, line), q)
        )
        copy.start()
        line_copies.append(copy)
    plane_copies = []

    def forward(i):
        source = at(lax.rem(l + line - i, line), q)
        for p in range(1, plane):
            copy = remote(
                spot(source),
                spot(source),
                gsend.at[i, p],
                grecv.at[i, p],
                at(l, lax.rem(q + p, plane)),
            )
            copy.start()
            plane_copies.append(copy)

    forward(0)

    shell_pick = (iota((LANES, PIXC), 0) == iota((LANES, PIXC), 1) // (PIXC // NSHELL)).astype(
        F32
    ).astype(BF16)
    inverse = jnp.broadcast_to(1.0 / sigma2[...], (8, NSHELL))
    noise[...] = exact(inverse, lambda v: dot(v, shell_pick[:NSHELL]))
    base = table[...]
    base = jnp.concatenate(
        [base, base, base, jnp.zeros((LANES - 3 * NBIN, PIXC), F32)], axis=0
    )
    tables[0] = by_group(base, 0)
    tables[1] = (base * base * noise[0:1, :]).astype(BF16)
    tables[2] = (base * base).astype(BF16)
    row = iota((LANES, count), 0)
    onehot[...] = (
        jnp.where((row < 3 * NBIN) & (lax.rem(row, NBIN) == bins[...]), 1.0, 0.0)
    ).astype(BF16)

    step = LANES

    def prepare(first, last):
        def body(i, carry):
            span = pl.ds(pl.multiple_of(i * step, step), step)
            picks = onehot[:, span]
            contrast = lax.dot_general(
                picks, tables[0], (((0,), (0,)), ((), ())), preferred_element_type=F32
            )
            level = noise[0:1, :]
            for part in range(2):
                cols = slice(part * PIXC, (part + 1) * PIXC)
                product = images[span, cols].astype(F32) * contrast
                centred[span, cols] = product.astype(BF16)
                weighted[span, cols] = (product * level).astype(BF16)
            return carry

        lax.fori_loop(first, last, body, 0)

    per = quarter // step
    for i in range(4):
        loads[i].wait()
        if i == 2:
            for s in range(1, line):
                line_copies[s].wait_recv()
                forward(s)
        prepare(i * per, (i + 1) * per)

    ids = jnp.broadcast_to(orient[...].astype(F32), (8, ORIENT)).astype(BF16)
    shape = (ORIENT, total_rows)
    col = iota(shape, 1)
    within = lax.rem(col, pad)
    expand = jnp.where(
        (col // block * rows + within == iota(shape, 0)) & (within < rows), 1.0, 0.0
    ).astype(BF16)
    ids_cols = dot(ids, expand)[0:1, :]
    square = (total_rows, total_rows)
    r = iota((total_rows, 1), 0)
    slot = lax.rem(r, pad)
    r_sub = lax.rem(r // block, line)
    r_kind = jnp.where(r_sub < line // 2, kind, 1 - kind)
    r_line = line_of(lax.rem(r_sub + pair, line // 2), r_kind)
    r_plane = lax.rem(r // own_rows + q, plane)
    owner = at(r_line, r_plane)
    pairs = n // 2
    direction = lax.rem(owner, pairs) * (2 * rows) + owner // pairs * rows + slot
    direction = jnp.where(slot < rows, direction, -1).astype(F32)
    c = iota((1, total_rows), 1)
    c_part = lax.rem(c // pad, 2)
    c_ok = lax.rem(c, pad) < rows
    real_ids = jnp.where(c_ok & (c_part == 0), ids_cols, -2.0)
    imag_ids = jnp.where(c_ok & (c_part == 1), ids_cols, -2.0)
    pick_real = jnp.where(jnp.broadcast_to(direction, square) == real_ids, 1.0, 0.0).astype(BF16)
    pick_imag = jnp.where(jnp.broadcast_to(direction, square) == imag_ids, 1.0, 0.0).astype(BF16)
    row_half = lax.rem(r // pad, 2)

    for copy in plane_copies:
        copy.wait_recv()
    whole = gathered[...]
    panel_real = dot(pick_real, whole)
    panel_imag = dot(pick_imag, whole)
    panel_power = (panel_real * panel_real + panel_imag * panel_imag).astype(BF16)
    norm = by_group(dot_t(panel_power, tables[1]), 1)
    scores = (
        dot_t(panel_real.astype(BF16), weighted[:, :PIXC])
        + dot_t(panel_imag.astype(BF16), weighted[:, PIXC:])
        - 0.5 * dot(norm, onehot[...])
    )
    use = (prior[...] > 0) & (halves[...] == row_half) & (slot < rows)
    masked = jnp.where(use, scores, -1e30)
    local_peak = jnp.max(masked, axis=0, keepdims=True)
    raw = jnp.where(use, jnp.exp(masked - local_peak), 0.0)
    local_total = jnp.sum(raw, axis=0, keepdims=True)
    peaks[0, 0:1, :] = local_peak
    peaks[0, 1:2, :] = local_total
    class_copies = []
    for i in range(1, ncls):
        copy = remote(
            peaks.at[0],
            peaks.at[i],
            csend.at[i],
            crecv.at[i],
            cls=lax.rem(mine + i, ncls),
        )
        copy.start()
        class_copies.append(copy)
    for copy in class_copies:
        copy.wait_recv()
    peak = local_peak
    for i in range(1, ncls):
        peak = jnp.maximum(peak, peaks[i, 0:1, :])
    total = local_total * jnp.exp(local_peak - peak)
    for i in range(1, ncls):
        total = total + peaks[i, 1:2, :] * jnp.exp(peaks[i, 0:1, :] - peak)
    posts[...] = (raw * (jnp.exp(local_peak - peak) / total)).astype(BF16)
    evidence[...] = peak + jnp.log(total)

    plane_sends, pair_sends, class_sends, swaps = [], [], [], []

    def launch(k):
        start, width = CHUNKS[k]
        data_width = min(width, 2 * PIXC - start)
        part = dot(posts[...], centred[:, start : start + data_width])
        acc[:, start : start + data_width] = part[:own_rows]
        send1[:, start : start + data_width] = part[own_rows:].astype(BF16)
        if data_width < width:
            sums = dot_t(posts[...], onehot[...])
            acc[:, 2 * PIXC :] = jnp.where(
                iota((own_rows, LANES), 1) < NBIN, sums[:own_rows], 0.0
            )
            send1[:, 2 * PIXC :] = by_group(sums[own_rows:], 1)
        cols = pl.ds(start, width)
        group = []
        for p in range(1, plane):
            copy = remote(
                send1.at[pl.ds((p - 1) * own_rows, own_rows), cols],
                recv1.at[p - 1, :, cols],
                s1send.at[k, p],
                s1recv.at[k, p],
                at(l, lax.rem(q + p, plane)),
            )
            copy.start()
            group.append(copy)
        plane_sends.append(group)

    def plane_sum(k):
        start, width = CHUNKS[k]
        cols = pl.ds(start, width)
        for copy in plane_sends[k]:
            copy.wait_recv()
        value = acc[:, start : start + width]
        for p in range(1, plane):
            value = value + recv1[p - 1, :, start : start + width].astype(F32)
        acc[:, start : start + width] = value
        copy = remote(
            acc.at[pl.ds(pair_rows, pair_rows), cols],
            recv2.at[:, cols],
            s2send.at[k, 0],
            s2recv.at[k, 0],
            at(l + 1 - 2 * lax.rem(l, 2), q),
        )
        copy.start()
        pair_sends.append(copy)

    def pair_sum(k):
        start, width = CHUNKS[k]
        cols = pl.ds(start, width)
        pair_sends[k].wait_recv()
        acc[:pair_rows, start : start + width] = (
            acc[:pair_rows, start : start + width] + recv2[:, start : start + width]
        )
        group = []
        for i in range(1, line // 2):
            copy = remote(
                acc.at[pl.ds(i * block, block), cols],
                recv3.at[i - 1, :, cols],
                s2send.at[k, i],
                s2recv.at[k, i],
                at(line_of(lax.rem(pair + i, line // 2), kind), q),
            )
            copy.start()
            group.append(copy)
        class_sends.append(group)

    def finish(k):
        start, width = CHUNKS[k]
        cols = pl.ds(start, width)
        for copy in class_sends[k]:
            copy.wait_recv()
        value = acc[:block, start : start + width]
        for i in range(1, line // 2):
            value = value + recv3[i - 1, :, start : start + width]
        first, second = value[:pad], value[pad:]
        final[0, :, start : start + width] = first
        final[1, :, start : start + width] = second
        copy = remote(
            final.at[1 - half, :, cols],
            swapped.at[half, :, cols],
            xsend.at[k],
            xrecv.at[k],
            lax.rem(me + n // 2, n),
        )
        copy.start()
        swaps.append(copy)
        for i, product in enumerate((first * second, first * first, second * second)):
            shells[i : i + 1, start : start + width] = jnp.sum(product, axis=0, keepdims=True)

    count_chunks = len(CHUNKS)
    for k in range(WINDOW):
        launch(k)
    for k in range(count_chunks + 2):
        if k < count_chunks:
            plane_sum(k)
        if k + WINDOW < count_chunks:
            launch(k + WINDOW)
        if 1 <= k <= count_chunks:
            pair_sum(k - 1)
        if k >= 2:
            finish(k - 2)

    table_rows = jnp.concatenate(
        [
            shells[0:3, :PIXC] + shells[0:3, PIXC : 2 * PIXC],
            jnp.zeros((5, PIXC), F32),
        ],
        axis=0,
    )
    stats[0] = exact(table_rows, lambda v: dot_t(v, shell_pick))
    stat_copies = []
    for i in range(1, n):
        copy = remote(
            stats.at[0], stats.at[i], tsend.at[i], trecv.at[i], lax.rem(me + i, n)
        )
        copy.start()
        stat_copies.append(copy)
    kept = final[half]
    for copy in swaps:
        copy.wait_recv()
    swapped[half] = kept
    ready = []
    for h in range(2):
        bin_sums = swapped[h, :, 2 * PIXC :]
        ready.append(1.0 + exact(bin_sums, lambda v: dot(v, tables[2])))
    for copy in stat_copies:
        copy.wait_recv()
    sums = stats[0]
    for i in range(1, n):
        sums = sums + stats[i]
    fsc = sums[0:1] / jnp.sqrt(sums[1:2] * sums[2:3] + 1e-06)
    factor = jnp.broadcast_to((1.0 + fsc) / 2.0, (8, LANES))
    factor = exact(factor, lambda v: dot(v, shell_pick))[0:1, :]
    for h in range(2):
        for part in range(2):
            cols = slice(part * PIXC, (part + 1) * PIXC)
            value = swapped[h, :, cols] * factor / ready[h]
            maps[0, h * rows : (h + 1) * rows, cols] = value[:rows]

    for copy in line_copies[1:] + plane_copies + class_copies + stat_copies:
        copy.wait_send()
    for copy in pair_sends + swaps:
        copy.wait_send()
    for group in plane_sends + class_sends:
        for copy in group:
            copy.wait_send()


def write_out(maps, evidence, maps_out, evidence_out, sems):
    first = pltpu.make_async_copy(maps, maps_out, sems.at[0])
    second = pltpu.make_async_copy(evidence, evidence_out, sems.at[1])
    first.start()
    second.start()
    first.wait()
    second.wait()


def solution(mesh):
    n = mesh.shape["ptcl"]
    ncls = mesh.shape["cls"]
    plane = 4
    line = n // plane
    rows = ORIENT // n
    pad = max(8, rows)
    block = 2 * pad
    own_rows = line * block
    nchunks = len(CHUNKS)

    def on_device(particles, panels, sigma2, defocus_bins, half_sets, prior_mask, orient_ids):
        count = particles.shape[0]
        dims = (n, ncls, plane, line, rows, pad, count)
        vmem = pl.BlockSpec(memory_space=pltpu.VMEM)
        hbm = pl.BlockSpec(memory_space=pl.ANY)
        dma = pltpu.SemaphoreType.DMA
        maps, evidence = pl.pallas_call(
            functools.partial(kernel, dims),
            out_shape=(
                jax.ShapeDtypeStruct((1, 2 * rows, 2 * PIXC), F32),
                jax.ShapeDtypeStruct((1, count), F32),
            ),
            in_specs=[hbm] + [vmem] * 7,
            out_specs=(vmem, vmem),
            scratch_shapes=[
                pltpu.VMEM((count, 2 * PIXC), BF16),
                pltpu.VMEM((count, 2 * PIXC), BF16),
                pltpu.VMEM((count, 2 * PIXC), BF16),
                pltpu.VMEM((n * block, PIXC), BF16),
                pltpu.VMEM((LANES, count), BF16),
                pltpu.VMEM((3, LANES, PIXC), BF16),
                pltpu.VMEM((8, PIXC), F32),
                pltpu.VMEM((ncls, 2, count), F32),
                pltpu.VMEM((n * block, count), BF16),
                pltpu.VMEM((n * block - own_rows, WIDTH), BF16),
                pltpu.VMEM((plane - 1, own_rows, WIDTH), BF16),
                pltpu.VMEM((own_rows, WIDTH), F32),
                pltpu.VMEM((own_rows // 2, WIDTH), F32),
                pltpu.VMEM((line // 2 - 1, block, WIDTH), F32),
                pltpu.VMEM((2, pad, WIDTH), F32),
                pltpu.VMEM((2, pad, WIDTH), F32),
                pltpu.VMEM((8, WIDTH), F32),
                pltpu.VMEM((n, 8, LANES), F32),
                dma((4,)),
                dma((line, plane)),
                dma((line, plane)),
                dma((ncls,)),
                dma((ncls,)),
                dma((nchunks, plane)),
                dma((nchunks, plane)),
                dma((nchunks, line)),
                dma((nchunks, line)),
                dma((nchunks,)),
                dma((nchunks,)),
                dma((n,)),
                dma((n,)),
            ],
            compiler_params=pltpu.CompilerParams(
                collective_id=0, has_side_effects=True, vmem_limit_bytes=56 * 2**20
            ),
        )(
            particles,
            panels,
            sigma2.reshape(1, NSHELL),
            defocus_bins.reshape(1, count),
            half_sets.reshape(1, count),
            prior_mask.reshape(1, count),
            orient_ids.reshape(1, ORIENT),
            jnp.asarray(ctf_table()),
        )
        maps, evidence = pl.pallas_call(
            write_out,
            out_shape=(
                jax.ShapeDtypeStruct(maps.shape, F32),
                jax.ShapeDtypeStruct(evidence.shape, F32),
            ),
            in_specs=[hbm, hbm],
            out_specs=(hbm, hbm),
            scratch_shapes=[dma((2,))],
        )(maps, evidence)
        return maps, evidence.reshape(count)

    return jax.shard_map(
        on_device,
        mesh=mesh,
        in_specs=(
            P("ptcl", None),
            P("cls", "ptcl", None),
            P(),
            P("ptcl"),
            P("ptcl"),
            P("ptcl", "cls"),
            P(),
        ),
        out_specs=(P("cls", "ptcl", None), P("ptcl")),
        check_vma=False,
    )
```

```python
import functools

import jax
import jax.numpy as jnp
import numpy as np
from jax import lax
from jax.experimental import pallas as pl
from jax.experimental.pallas import tpu as pltpu
from jax.sharding import PartitionSpec as P

PIXC = 1024
ORIENT = 128
NSHELL = 32
NBIN = 16
LANES = 128
WIDTH = 2 * PIXC + LANES
TILES = WIDTH // LANES
DATA_TILES = TILES - 1
CHUNKS = ((12, 5), (0, 4), (4, 4), (8, 2), (10, 2))
WINDOW = 2
MESH = pl.DeviceIdType.MESH
BF16 = jnp.bfloat16
F32 = jnp.float32


def ctf_table():
    defocus = (np.arange(NBIN, dtype=np.float32) + np.float32(1.0)) / np.float32(NBIN)
    radius = (np.arange(PIXC, dtype=np.float32) + np.float32(0.5)) / np.float32(PIXC)
    phase = np.float32(0.3) + np.float32(2.5) * defocus[:, None] * radius[None, :]
    wide = phase.astype(np.float64)
    return (np.sin(wide) + 0.1 * np.cos(wide)).astype(np.float32)


def iota(shape, dim):
    return lax.broadcasted_iota(jnp.int32, shape, dim)


def over(values, size):
    return lax.shift_right_logical(values, jnp.int32(size.bit_length() - 1))


def mod(values, size):
    return lax.bitwise_and(values, jnp.int32(size - 1))


def dot(left, right):
    return lax.dot_general(left, right, (((1,), (0,)), ((), ())), preferred_element_type=F32)


def dot_t(left, right):
    return lax.dot_general(left, right, (((1,), (1,)), ((), ())), preferred_element_type=F32)


def split3(values):
    high = values.astype(BF16)
    rest = values - high.astype(F32)
    mid = rest.astype(BF16)
    low = (rest - mid.astype(F32)).astype(BF16)
    return high, mid, low


def exact(values, product):
    high, mid, low = split3(values)
    return product(high) + product(mid) + product(low)


def by_group(values, dim):
    high, mid, low = split3(values)
    axis = [1, 1]
    axis[dim] = values.shape[dim]
    group = over(iota(tuple(axis), dim), NBIN)
    mixed = jnp.where(
        group == 0,
        high.astype(F32),
        jnp.where(group == 1, mid.astype(F32), jnp.where(group == 2, low.astype(F32), 0.0)),
    )
    return mixed.astype(BF16)


def kernel(
    dims,
    particles,
    panels,
    sigma2,
    bins,
    halves,
    prior,
    orient,
    table,
    maps,
    evidence,
    images,
    weighted,
    centred,
    gathered,
    onehot,
    tables,
    noise,
    peaks,
    posts,
    send1,
    recv1,
    acc,
    recv2,
    recv3,
    final,
    swapped,
    shells,
    stats,
    load_sem,
    gsend,
    grecv,
    csend,
    crecv,
    s1send,
    s1recv,
    s2send,
    s2recv,
    xsend,
    xrecv,
    tsend,
    trecv,
):
    n, ncls, plane, line, rows, pad, count = dims
    block = 2 * pad
    total_rows = n * block
    own_rows = line * block
    me = lax.axis_index("ptcl")
    mine = lax.axis_index("cls")
    q = lax.rem(me, plane)
    l = me // plane
    half = me // (n // 2)

    pair = l // 2
    kind = lax.rem(l + pair, 2)

    def line_of(pair_pos, wanted):
        return 2 * pair_pos + lax.rem(pair_pos + wanted, 2)

    def at(line_pos, plane_pos):
        return line_pos * plane + plane_pos

    def remote(src, dst, send, recv, ptcl=None, cls=None):
        return pltpu.make_async_remote_copy(
            src_ref=src,
            dst_ref=dst,
            send_sem=send,
            recv_sem=recv,
            device_id=(mine if cls is None else cls, me if ptcl is None else ptcl),
            device_id_type=MESH,
        )

    barrier = pltpu.get_barrier_semaphore()
    for i in range(1, n):
        pl.semaphore_signal(
            barrier, inc=1, device_id=(mine, lax.rem(me + i, n)), device_id_type=MESH
        )
    for i in range(1, ncls):
        pl.semaphore_signal(
            barrier, inc=1, device_id=(lax.rem(mine + i, ncls), me), device_id_type=MESH
        )
    quarter = count // 4
    loads = []
    for i in range(4):
        span = pl.ds(i * quarter, quarter)
        loads.append(
            pltpu.make_async_copy(particles.at[span], images.at[span], load_sem.at[i])
        )
        loads[-1].start()

    piece = panels[0].astype(F32)
    real, imag = piece[:, :PIXC], piece[:, PIXC:]
    if rows < pad:
        fill = jnp.zeros((pad - rows, PIXC), F32)
        parts = [real, fill, imag, fill]
    else:
        parts = [real, imag]

    def spot(device):
        return gathered.at[pl.ds(pl.multiple_of(device * block, block), block)]

    gathered[pl.ds(pl.multiple_of(me * block, block), block), :] = jnp.concatenate(
        parts, axis=0
    ).astype(BF16)
    pl.semaphore_wait(barrier, n - 1 + ncls - 1)

    sends = []
    line_copies = [None]
    for i in range(1, line):
        copy = remote(
            spot(me), spot(me), gsend.at[i, 0], grecv.at[i, 0], at(lax.rem(l + i, line), q)
        )
        copy.start()
        line_copies.append(copy)
    plane_copies = []

    def forward(i):
        source = at(lax.rem(l + line - i, line), q)
        for p in range(1, plane):
            copy = remote(
                spot(source),
                spot(source),
                gsend.at[i, p],
                grecv.at[i, p],
                at(l, lax.rem(q + p, plane)),
            )
            copy.start()
            plane_copies.append(copy)

    forward(0)

    shell_pick = (iota((LANES, 1), 0) == over(iota((1, PIXC), 1), PIXC // NSHELL)).astype(
        F32
    ).astype(BF16)
    inverse = jnp.broadcast_to(1.0 / sigma2[...], (8, NSHELL))
    noise[...] = exact(inverse, lambda v: dot(v, shell_pick[:NSHELL]))
    base = table[...]
    base = jnp.concatenate(
        [base, base, base, jnp.zeros((LANES - 3 * NBIN, PIXC), F32)], axis=0
    )
    tables[0] = by_group(base, 0)
    tables[1] = (base * base * noise[0:1, :]).astype(BF16)
    tables[2] = (base * base).astype(BF16)
    row = iota((LANES, 1), 0)
    row = jnp.where(row < 3 * NBIN, mod(row, NBIN), -1)
    onehot[...] = (
        jnp.where(row == bins[...], 1.0, 0.0)
    ).astype(BF16)

    step = LANES

    def prepare(first, last):
        def body(i, carry):
            span = pl.ds(pl.multiple_of(i * step, step), step)
            picks = onehot[:, span]
            contrast = lax.dot_general(
                picks, tables[0], (((0,), (0,)), ((), ())), preferred_element_type=F32
            )
            level = noise[0:1, :]
            for part in range(2):
                cols = slice(part * PIXC, (part + 1) * PIXC)
                product = images[span, cols].astype(F32) * contrast
                centred[span, cols] = product.astype(BF16)
                weighted[span, cols] = (product * level).astype(BF16)
            return carry

        lax.fori_loop(first, last, body, 0)

    per = quarter // step
    for i in range(4):
        loads[i].wait()
        for s in range(1, line):
            if min(s, 3) == i:
                line_copies[s].wait_recv()
                forward(s)
        prepare(i * per, (i + 1) * per)

    ids = jnp.broadcast_to(orient[...].astype(F32), (8, ORIENT)).astype(BF16)
    c = iota((1, total_rows), 1)
    c_slot = mod(c, pad)
    c_part = mod(over(c, pad), 2)
    source_id = jnp.where(c_slot < rows, over(c, block) * rows + c_slot, -1)
    expand = jnp.where(source_id == iota((ORIENT, 1), 0), 1.0, 0.0).astype(BF16)
    ids_cols = dot(ids, expand)[0:1, :]
    square = (total_rows, total_rows)
    r = iota((total_rows, 1), 0)
    slot = mod(r, pad)
    r_sub = mod(over(r, block), line)
    r_kind = jnp.where(r_sub < line // 2, kind, 1 - kind)
    r_pair = mod(r_sub + pair, line // 2)
    r_line = 2 * r_pair + mod(r_pair + r_kind, 2)
    r_plane = mod(over(r, own_rows) + q, plane)
    owner = at(r_line, r_plane)
    pairs = n // 2
    direction = mod(owner, pairs) * (2 * rows) + over(owner, pairs) * rows + slot
    direction = jnp.where(slot < rows, direction, -1).astype(F32)
    c_ok = c_slot < rows
    real_ids = jnp.where(c_ok & (c_part == 0), ids_cols, -2.0)
    imag_ids = jnp.where(c_ok & (c_part == 1), ids_cols, -2.0)
    pick_real = jnp.where(jnp.broadcast_to(direction, square) == real_ids, 1.0, 0.0).astype(BF16)
    pick_imag = jnp.where(jnp.broadcast_to(direction, square) == imag_ids, 1.0, 0.0).astype(BF16)
    row_half = mod(over(r, pad), 2)

    for copy in plane_copies:
        copy.wait_recv()
    whole = gathered[...]
    panel_real = dot(pick_real, whole)
    panel_imag = dot(pick_imag, whole)
    panel_power = (panel_real * panel_real + panel_imag * panel_imag).astype(BF16)
    norm = by_group(dot_t(panel_power, tables[1]), 1)
    scores = (
        dot_t(panel_real.astype(BF16), weighted[:, :PIXC])
        + dot_t(panel_imag.astype(BF16), weighted[:, PIXC:])
        - 0.5 * dot(norm, onehot[...])
    )
    use = (prior[...] > 0) & (halves[...] == row_half) & (slot < rows)
    masked = jnp.where(use, scores, -1e30)
    local_peak = jnp.max(masked, axis=0, keepdims=True)
    raw = jnp.where(use, jnp.exp(masked - local_peak), 0.0)
    local_total = jnp.sum(raw, axis=0, keepdims=True)
    peaks[0, 0:1, :] = local_peak
    peaks[0, 1:2, :] = local_total
    class_copies = []
    for i in range(1, ncls):
        copy = remote(
            peaks.at[0],
            peaks.at[i],
            csend.at[i],
            crecv.at[i],
            cls=lax.rem(mine + i, ncls),
        )
        copy.start()
        class_copies.append(copy)
    for copy in class_copies:
        copy.wait_recv()
    peak = local_peak
    for i in range(1, ncls):
        peak = jnp.maximum(peak, peaks[i, 0:1, :])
    total = local_total * jnp.exp(local_peak - peak)
    for i in range(1, ncls):
        total = total + peaks[i, 1:2, :] * jnp.exp(peaks[i, 0:1, :] - peak)
    posts[...] = (raw * (jnp.exp(local_peak - peak) / total)).astype(BF16)
    evidence[...] = peak + jnp.log(total)

    plane_sends, pair_sends, class_sends, swaps = [], [], [], []

    def launch(k):
        first, tiles = CHUNKS[k]
        data_tiles = min(tiles, DATA_TILES - first)
        start = first * LANES
        part = dot(posts[...], centred[:, start : start + data_tiles * LANES])
        for t in range(data_tiles):
            lanes = slice(t * LANES, (t + 1) * LANES)
            for i in range(line):
                acc[i, first + t] = part[i * block : (i + 1) * block, lanes]
            for p in range(1, plane):
                send1[p - 1, first + t] = part[
                    p * own_rows : (p + 1) * own_rows, lanes
                ].astype(BF16)
        if data_tiles < tiles:
            sums = dot_t(posts[...], onehot[...])
            kept = jnp.where(iota((1, LANES), 1) < NBIN, sums[:own_rows], 0.0)
            for i in range(line):
                acc[i, DATA_TILES] = kept[i * block : (i + 1) * block]
            for p in range(1, plane):
                send1[p - 1, DATA_TILES] = by_group(sums[p * own_rows : (p + 1) * own_rows], 1)
        span = pl.ds(first, tiles)
        group = []
        for p in range(1, plane):
            copy = remote(
                send1.at[p - 1, span],
                recv1.at[p - 1, span],
                s1send.at[k, p],
                s1recv.at[k, p],
                at(l, lax.rem(q + p, plane)),
            )
            copy.start()
            group.append(copy)
        plane_sends.append(group)

    def plane_sum(k):
        first, tiles = CHUNKS[k]
        span = pl.ds(first, tiles)
        for copy in plane_sends[k]:
            copy.wait_recv()
        for t in range(first, first + tiles):
            value = recv1[0, t].astype(F32)
            for p in range(2, plane):
                value = value + recv1[p - 1, t].astype(F32)
            for i in range(line):
                acc[i, t] = acc[i, t] + value[i * block : (i + 1) * block]
        copy = remote(
            acc.at[pl.ds(line // 2, line // 2), span],
            recv2.at[:, span],
            s2send.at[k, 0],
            s2recv.at[k, 0],
            at(l + 1 - 2 * lax.rem(l, 2), q),
        )
        copy.start()
        pair_sends.append(copy)

    def pair_sum(k):
        first, tiles = CHUNKS[k]
        span = pl.ds(first, tiles)
        pair_sends[k].wait_recv()
        for i in range(line // 2):
            acc[i, first : first + tiles] = (
                acc[i, first : first + tiles] + recv2[i, first : first + tiles]
            )
        group = []
        for i in range(1, line // 2):
            copy = remote(
                acc.at[i, span],
                recv3.at[i - 1, span],
                s2send.at[k, i],
                s2recv.at[k, i],
                at(line_of(lax.rem(pair + i, line // 2), kind), q),
            )
            copy.start()
            group.append(copy)
        class_sends.append(group)

    def finish(k):
        first, tiles = CHUNKS[k]
        span = pl.ds(first, tiles)
        for copy in class_sends[k]:
            copy.wait_recv()
        for t in range(first, first + tiles):
            value = acc[0, t]
            for i in range(1, line // 2):
                value = value + recv3[i - 1, t]
            zero, one = value[:pad], value[pad:]
            final[0, t] = zero
            final[1, t] = one
            lanes = slice(t * LANES, (t + 1) * LANES)
            for i, product in enumerate((zero * one, zero * zero, one * one)):
                shells[i : i + 1, lanes] = jnp.sum(product, axis=0, keepdims=True)
        copy = remote(
            final.at[1 - half, span],
            swapped.at[half, span],
            xsend.at[k],
            xrecv.at[k],
            lax.rem(me + n // 2, n),
        )
        copy.start()
        swaps.append(copy)

    count_chunks = len(CHUNKS)
    for k in range(WINDOW):
        launch(k)
    for k in range(count_chunks + 2):
        if k < count_chunks:
            plane_sum(k)
        if k + WINDOW < count_chunks:
            launch(k + WINDOW)
        if 1 <= k <= count_chunks:
            pair_sum(k - 1)
        if k >= 2:
            finish(k - 2)

    table_rows = jnp.concatenate(
        [
            shells[0:3, :PIXC] + shells[0:3, PIXC : 2 * PIXC],
            jnp.zeros((5, PIXC), F32),
        ],
        axis=0,
    )
    stats[0] = exact(table_rows, lambda v: dot_t(v, shell_pick))
    stat_copies = []
    for i in range(1, n):
        copy = remote(
            stats.at[0], stats.at[i], tsend.at[i], trecv.at[i], lax.rem(me + i, n)
        )
        copy.start()
        stat_copies.append(copy)
    kept = final[half]
    for copy in swaps:
        copy.wait_recv()
    swapped[half] = kept
    ready = []
    for h in range(2):
        bin_sums = swapped[h, DATA_TILES]
        ready.append(1.0 + exact(bin_sums, lambda v: dot(v, tables[2])))
    for copy in stat_copies:
        copy.wait_recv()
    sums = stats[0]
    for i in range(1, n):
        sums = sums + stats[i]
    fsc = sums[0:1] / jnp.sqrt(sums[1:2] * sums[2:3] + 1e-06)
    factor = jnp.broadcast_to((1.0 + fsc) / 2.0, (8, LANES))
    factor = exact(factor, lambda v: dot(v, shell_pick))[0:1, :]
    for h in range(2):
        scale = factor / ready[h]
        for t in range(DATA_TILES):
            lanes = slice(t * LANES, (t + 1) * LANES)
            k = t % (PIXC // LANES)
            value = swapped[h, t] * scale[:, k * LANES : (k + 1) * LANES]
            maps[0, h * rows : (h + 1) * rows, lanes] = value[:rows]

    for copy in line_copies[1:] + plane_copies + class_copies + stat_copies:
        copy.wait_send()
    for copy in pair_sends + swaps:
        copy.wait_send()
    for group in plane_sends + class_sends:
        for copy in group:
            copy.wait_send()


def write_out(maps, evidence, maps_out, evidence_out):
    maps_out[...] = maps[...]
    evidence_out[...] = evidence[...]


def solution(mesh):
    n = mesh.shape["ptcl"]
    ncls = mesh.shape["cls"]
    plane = 4
    line = n // plane
    rows = ORIENT // n
    pad = max(8, rows)
    block = 2 * pad
    own_rows = line * block
    nchunks = len(CHUNKS)

    def on_device(particles, panels, sigma2, defocus_bins, half_sets, prior_mask, orient_ids):
        count = particles.shape[0]
        dims = (n, ncls, plane, line, rows, pad, count)
        vmem = pl.BlockSpec(memory_space=pltpu.VMEM)
        hbm = pl.BlockSpec(memory_space=pltpu.HBM)
        dma = pltpu.SemaphoreType.DMA
        maps, evidence = pl.pallas_call(
            functools.partial(kernel, dims),
            out_shape=(
                jax.ShapeDtypeStruct((1, 2 * rows, 2 * PIXC), F32),
                jax.ShapeDtypeStruct((1, count), F32),
            ),
            in_specs=[hbm] + [vmem] * 7,
            out_specs=(vmem, vmem),
            scratch_shapes=[
                pltpu.VMEM((count, 2 * PIXC), BF16),
                pltpu.VMEM((count, 2 * PIXC), BF16),
                pltpu.VMEM((count, 2 * PIXC), BF16),
                pltpu.VMEM((n * block, PIXC), BF16),
                pltpu.VMEM((LANES, count), BF16),
                pltpu.VMEM((3, LANES, PIXC), BF16),
                pltpu.VMEM((8, PIXC), F32),
                pltpu.VMEM((ncls, 2, count), F32),
                pltpu.VMEM((n * block, count), BF16),
                pltpu.VMEM((plane - 1, TILES, own_rows, LANES), BF16),
                pltpu.VMEM((plane - 1, TILES, own_rows, LANES), BF16),
                pltpu.VMEM((line, TILES, block, LANES), F32),
                pltpu.VMEM((line // 2, TILES, block, LANES), F32),
                pltpu.VMEM((line // 2 - 1, TILES, block, LANES), F32),
                pltpu.VMEM((2, TILES, pad, LANES), F32),
                pltpu.VMEM((2, TILES, pad, LANES), F32),
                pltpu.VMEM((8, WIDTH), F32),
                pltpu.VMEM((n, 8, LANES), F32),
                dma((4,)),
                dma((line, plane)),
                dma((line, plane)),
                dma((ncls,)),
                dma((ncls,)),
                dma((nchunks, plane)),
                dma((nchunks, plane)),
                dma((nchunks, line)),
                dma((nchunks, line)),
                dma((nchunks,)),
                dma((nchunks,)),
                dma((n,)),
                dma((n,)),
            ],
            compiler_params=pltpu.CompilerParams(
                collective_id=0, has_side_effects=True, vmem_limit_bytes=58 * 2**20
            ),
        )(
            particles,
            panels,
            sigma2.reshape(1, NSHELL),
            defocus_bins.reshape(1, count),
            half_sets.reshape(1, count),
            prior_mask.reshape(1, count),
            orient_ids.reshape(1, ORIENT),
            jnp.asarray(ctf_table()),
        )
        maps, evidence = pl.pallas_call(
            write_out,
            out_shape=(
                jax.ShapeDtypeStruct(maps.shape, F32),
                jax.ShapeDtypeStruct(evidence.shape, F32),
            ),
            in_specs=[vmem, vmem],
            out_specs=(vmem, vmem),
        )(maps, evidence)
        return maps, evidence.reshape(count)

    return jax.shard_map(
        on_device,
        mesh=mesh,
        in_specs=(
            P("ptcl", None),
            P("cls", "ptcl", None),
            P(),
            P("ptcl"),
            P("ptcl"),
            P("ptcl", "cls"),
            P(),
        ),
        out_specs=(P("cls", "ptcl", None), P("ptcl")),
        check_vma=False,
    )
```

```python
import functools

import jax
import jax.numpy as jnp
import numpy as np
from jax import lax
from jax.experimental import pallas as pl
from jax.experimental.pallas import tpu as pltpu
from jax.sharding import PartitionSpec as P

PIXC = 1024
ORIENT = 128
NSHELL = 32
NBIN = 16
LANES = 128
WIDTH = 2 * PIXC + LANES
TILES = WIDTH // LANES
DATA_TILES = TILES - 1
CHUNKS = ((12, 5), (0, 4), (4, 4), (8, 2), (10, 2))
HALVES = 2
MESH = pl.DeviceIdType.MESH
BF16 = jnp.bfloat16
F32 = jnp.float32


def ctf_table():
    defocus = (np.arange(NBIN, dtype=np.float32) + np.float32(1.0)) / np.float32(NBIN)
    radius = (np.arange(PIXC, dtype=np.float32) + np.float32(0.5)) / np.float32(PIXC)
    phase = np.float32(0.3) + np.float32(2.5) * defocus[:, None] * radius[None, :]
    wide = phase.astype(np.float64)
    return (np.sin(wide) + 0.1 * np.cos(wide)).astype(np.float32)


def iota(shape, dim):
    return lax.broadcasted_iota(jnp.int32, shape, dim)


def over(values, size):
    return lax.shift_right_logical(values, jnp.int32(size.bit_length() - 1))


def mod(values, size):
    return lax.bitwise_and(values, jnp.int32(size - 1))


def dot(left, right):
    return lax.dot_general(left, right, (((1,), (0,)), ((), ())), preferred_element_type=F32)


def dot_t(left, right):
    return lax.dot_general(left, right, (((1,), (1,)), ((), ())), preferred_element_type=F32)


def split3(values):
    high = values.astype(BF16)
    rest = values - high.astype(F32)
    mid = rest.astype(BF16)
    low = (rest - mid.astype(F32)).astype(BF16)
    return high, mid, low


def exact(values, product):
    high, mid, low = split3(values)
    return product(high) + product(mid) + product(low)


def by_group(values, dim):
    high, mid, low = split3(values)
    axis = [1, 1]
    axis[dim] = values.shape[dim]
    group = over(iota(tuple(axis), dim), NBIN)
    mixed = jnp.where(
        group == 0,
        high.astype(F32),
        jnp.where(group == 1, mid.astype(F32), jnp.where(group == 2, low.astype(F32), 0.0)),
    )
    return mixed.astype(BF16)


def kernel(
    dims,
    particles,
    panels,
    sigma2,
    bins,
    halves,
    prior,
    orient,
    table,
    maps,
    evidence,
    images,
    weighted,
    centred,
    gathered,
    onehot,
    tables,
    noise,
    peaks,
    raw,
    posts,
    send1,
    recv1,
    acc,
    recv2,
    recv3,
    final,
    swapped,
    shells,
    stats,
    load_sem,
    gsend,
    grecv,
    csend,
    crecv,
    s1send,
    s1recv,
    s2send,
    s2recv,
    xsend,
    xrecv,
    tsend,
    trecv,
):
    n, ncls, plane, line, rows, pad, count = dims
    block = 2 * pad
    total_rows = n * block
    own_rows = line * block
    me = lax.axis_index("ptcl")
    mine = lax.axis_index("cls")
    q = lax.rem(me, plane)
    l = me // plane
    half = me // (n // 2)

    pair = l // 2
    kind = lax.rem(l + pair, 2)

    def line_of(pair_pos, wanted):
        return 2 * pair_pos + lax.rem(pair_pos + wanted, 2)

    def at(line_pos, plane_pos):
        return line_pos * plane + plane_pos

    def remote(src, dst, send, recv, ptcl=None, cls=None):
        return pltpu.make_async_remote_copy(
            src_ref=src,
            dst_ref=dst,
            send_sem=send,
            recv_sem=recv,
            device_id=(mine if cls is None else cls, me if ptcl is None else ptcl),
            device_id_type=MESH,
        )

    barrier = pltpu.get_barrier_semaphore()
    for i in range(1, n):
        pl.semaphore_signal(
            barrier, inc=1, device_id=(mine, lax.rem(me + i, n)), device_id_type=MESH
        )
    for i in range(1, ncls):
        pl.semaphore_signal(
            barrier, inc=1, device_id=(lax.rem(mine + i, ncls), me), device_id_type=MESH
        )
    quarter = count // 4
    loads = []
    for i in range(4):
        span = pl.ds(i * quarter, quarter)
        loads.append(
            pltpu.make_async_copy(particles.at[span], images.at[span], load_sem.at[i])
        )
        loads[-1].start()

    piece = panels[0].astype(F32)
    real, imag = piece[:, :PIXC], piece[:, PIXC:]
    if rows < pad:
        fill = jnp.zeros((pad - rows, PIXC), F32)
        parts = [real, fill, imag, fill]
    else:
        parts = [real, imag]

    def spot(device):
        return gathered.at[pl.ds(pl.multiple_of(device * block, block), block)]

    gathered[pl.ds(pl.multiple_of(me * block, block), block), :] = jnp.concatenate(
        parts, axis=0
    ).astype(BF16)
    pl.semaphore_wait(barrier, n - 1 + ncls - 1)

    sends = []
    line_copies = [None]
    for i in range(1, line):
        copy = remote(
            spot(me), spot(me), gsend.at[i, 0], grecv.at[i, 0], at(lax.rem(l + i, line), q)
        )
        copy.start()
        line_copies.append(copy)
    plane_copies = []

    def forward(i):
        source = at(lax.rem(l + line - i, line), q)
        for p in range(1, plane):
            copy = remote(
                spot(source),
                spot(source),
                gsend.at[i, p],
                grecv.at[i, p],
                at(l, lax.rem(q + p, plane)),
            )
            copy.start()
            plane_copies.append(copy)

    forward(0)

    shell_pick = (iota((LANES, 1), 0) == over(iota((1, PIXC), 1), PIXC // NSHELL)).astype(
        F32
    ).astype(BF16)
    inverse = jnp.broadcast_to(1.0 / sigma2[...], (8, NSHELL))
    noise[...] = exact(inverse, lambda v: dot(v, shell_pick[:NSHELL]))
    base = table[...]
    base = jnp.concatenate(
        [base, base, base, jnp.zeros((LANES - 3 * NBIN, PIXC), F32)], axis=0
    )
    tables[0] = by_group(base, 0)
    tables[1] = (base * base * noise[0:1, :]).astype(BF16)
    tables[2] = (base * base).astype(BF16)
    row = iota((LANES, 1), 0)
    row = jnp.where(row < 3 * NBIN, mod(row, NBIN), -1)
    onehot[...] = (
        jnp.where(row == bins[...], 1.0, 0.0)
    ).astype(BF16)

    step = LANES

    def prepare(first, last):
        def body(i, carry):
            span = pl.ds(pl.multiple_of(i * step, step), step)
            picks = onehot[:, span]
            contrast = lax.dot_general(
                picks, tables[0], (((0,), (0,)), ((), ())), preferred_element_type=F32
            )
            level = noise[0:1, :]
            for part in range(2):
                cols = slice(part * PIXC, (part + 1) * PIXC)
                product = images[span, cols].astype(F32) * contrast
                centred[span, cols] = product.astype(BF16)
                weighted[span, cols] = (product * level).astype(BF16)
            return carry

        lax.fori_loop(first, last, body, 0)

    per = quarter // step
    for i in range(4):
        loads[i].wait()
        for s in range(1, line):
            if min(s, 3) == i:
                line_copies[s].wait_recv()
                forward(s)
        prepare(i * per, (i + 1) * per)

    ids = jnp.broadcast_to(orient[...].astype(F32), (8, ORIENT)).astype(BF16)
    c = iota((1, total_rows), 1)
    c_slot = mod(c, pad)
    c_part = mod(over(c, pad), 2)
    source_id = jnp.where(c_slot < rows, over(c, block) * rows + c_slot, -1)
    expand = jnp.where(source_id == iota((ORIENT, 1), 0), 1.0, 0.0).astype(BF16)
    ids_cols = dot(ids, expand)[0:1, :]
    square = (total_rows, total_rows)
    r = iota((total_rows, 1), 0)
    slot = mod(r, pad)
    r_sub = mod(over(r, block), line)
    r_kind = jnp.where(r_sub < line // 2, kind, 1 - kind)
    r_pair = mod(r_sub + pair, line // 2)
    r_line = 2 * r_pair + mod(r_pair + r_kind, 2)
    r_plane = mod(over(r, own_rows) + q, plane)
    owner = at(r_line, r_plane)
    pairs = n // 2
    direction = mod(owner, pairs) * (2 * rows) + over(owner, pairs) * rows + slot
    direction = jnp.where(slot < rows, direction, -1).astype(F32)
    c_ok = c_slot < rows
    real_ids = jnp.where(c_ok & (c_part == 0), ids_cols, -2.0)
    imag_ids = jnp.where(c_ok & (c_part == 1), ids_cols, -2.0)
    pick_real = jnp.where(jnp.broadcast_to(direction, square) == real_ids, 1.0, 0.0).astype(BF16)
    pick_imag = jnp.where(jnp.broadcast_to(direction, square) == imag_ids, 1.0, 0.0).astype(BF16)
    row_half = mod(over(r, pad), 2)

    for copy in plane_copies:
        copy.wait_recv()
    whole = gathered[...]
    panel_real = dot(pick_real, whole)
    panel_imag = dot(pick_imag, whole)
    panel_power = (panel_real * panel_real + panel_imag * panel_imag).astype(BF16)
    norm = by_group(dot_t(panel_power, tables[1]), 1)
    panel_real = panel_real.astype(BF16)
    panel_imag = panel_imag.astype(BF16)
    valid = slot < rows
    class_copies = []
    lanes_each = count // HALVES
    for g in range(HALVES):
        span = slice(g * lanes_each, (g + 1) * lanes_each)
        scores = (
            dot_t(panel_real, weighted[span, :PIXC])
            + dot_t(panel_imag, weighted[span, PIXC:])
            - 0.5 * dot(norm, onehot[:, span])
        )
        use = (prior[:, span] > 0) & (halves[:, span] == row_half) & valid
        masked = jnp.where(use, scores, -1e30)
        local_peak = jnp.max(masked, axis=0, keepdims=True)
        value = jnp.where(use, jnp.exp(masked - local_peak), 0.0)
        raw[:, span] = value
        peaks[0, g, 0:1, :] = local_peak
        peaks[0, g, 1:2, :] = jnp.sum(value, axis=0, keepdims=True)
        group = []
        for i in range(1, ncls):
            copy = remote(
                peaks.at[0, g],
                peaks.at[i, g],
                csend.at[g, i],
                crecv.at[g, i],
                cls=lax.rem(mine + i, ncls),
            )
            copy.start()
            group.append(copy)
        class_copies.append(group)
    for g in range(HALVES):
        span = slice(g * lanes_each, (g + 1) * lanes_each)
        for copy in class_copies[g]:
            copy.wait_recv()
        local_peak = peaks[0, g, 0:1, :]
        peak = local_peak
        for i in range(1, ncls):
            peak = jnp.maximum(peak, peaks[i, g, 0:1, :])
        total = jnp.zeros_like(peak)
        for i in range(ncls):
            total = total + peaks[i, g, 1:2, :] * jnp.exp(peaks[i, g, 0:1, :] - peak)
        posts[:, span] = (raw[:, span] * (jnp.exp(local_peak - peak) / total)).astype(BF16)
        evidence[:, span] = peak + jnp.log(total)

    plane_sends, pair_sends, class_sends, swaps = [], [], [], []

    def launch(k):
        first, tiles = CHUNKS[k]
        data_tiles = min(tiles, DATA_TILES - first)
        start = first * LANES
        part = dot(posts[...], centred[:, start : start + data_tiles * LANES])
        for t in range(data_tiles):
            lanes = slice(t * LANES, (t + 1) * LANES)
            for i in range(line):
                acc[i, first + t] = part[i * block : (i + 1) * block, lanes]
            for p in range(1, plane):
                send1[p - 1, first + t] = part[
                    p * own_rows : (p + 1) * own_rows, lanes
                ].astype(BF16)
        if data_tiles < tiles:
            sums = dot_t(posts[...], onehot[...])
            kept = jnp.where(iota((1, LANES), 1) < NBIN, sums[:own_rows], 0.0)
            for i in range(line):
                acc[i, DATA_TILES] = kept[i * block : (i + 1) * block]
            for p in range(1, plane):
                send1[p - 1, DATA_TILES] = by_group(sums[p * own_rows : (p + 1) * own_rows], 1)
        span = pl.ds(first, tiles)
        group = []
        for p in range(1, plane):
            copy = remote(
                send1.at[p - 1, span],
                recv1.at[p - 1, span],
                s1send.at[k, p],
                s1recv.at[k, p],
                at(l, lax.rem(q + p, plane)),
            )
            copy.start()
            group.append(copy)
        plane_sends.append(group)

    def plane_sum(k):
        first, tiles = CHUNKS[k]
        span = pl.ds(first, tiles)
        for copy in plane_sends[k]:
            copy.wait_recv()
        for t in range(first, first + tiles):
            value = recv1[0, t].astype(F32)
            for p in range(2, plane):
                value = value + recv1[p - 1, t].astype(F32)
            for i in range(line):
                acc[i, t] = acc[i, t] + value[i * block : (i + 1) * block]
        copy = remote(
            acc.at[pl.ds(line // 2, line // 2), span],
            recv2.at[:, span],
            s2send.at[k, 0],
            s2recv.at[k, 0],
            at(l + 1 - 2 * lax.rem(l, 2), q),
        )
        copy.start()
        pair_sends.append(copy)

    def pair_sum(k):
        first, tiles = CHUNKS[k]
        span = pl.ds(first, tiles)
        pair_sends[k].wait_recv()
        for i in range(line // 2):
            acc[i, first : first + tiles] = (
                acc[i, first : first + tiles] + recv2[i, first : first + tiles]
            )
        group = []
        for i in range(1, line // 2):
            copy = remote(
                acc.at[i, span],
                recv3.at[i - 1, span],
                s2send.at[k, i],
                s2recv.at[k, i],
                at(line_of(lax.rem(pair + i, line // 2), kind), q),
            )
            copy.start()
            group.append(copy)
        class_sends.append(group)

    def finish(k):
        first, tiles = CHUNKS[k]
        span = pl.ds(first, tiles)
        for copy in class_sends[k]:
            copy.wait_recv()
        for t in range(first, first + tiles):
            value = acc[0, t]
            for i in range(1, line // 2):
                value = value + recv3[i - 1, t]
            zero, one = value[:pad], value[pad:]
            final[0, t] = zero
            final[1, t] = one
            lanes = slice(t * LANES, (t + 1) * LANES)
            for i, product in enumerate((zero * one, zero * zero, one * one)):
                shells[i : i + 1, lanes] = jnp.sum(product, axis=0, keepdims=True)
        copy = remote(
            final.at[1 - half, span],
            swapped.at[half, span],
            xsend.at[k],
            xrecv.at[k],
            lax.rem(me + n // 2, n),
        )
        copy.start()
        swaps.append(copy)

    count_chunks = len(CHUNKS)
    for k in range(count_chunks):
        launch(k)
    for k in range(count_chunks + 2):
        if k < count_chunks:
            plane_sum(k)
        if 1 <= k <= count_chunks:
            pair_sum(k - 1)
        if k >= 2:
            finish(k - 2)

    table_rows = jnp.concatenate(
        [
            shells[0:3, :PIXC] + shells[0:3, PIXC : 2 * PIXC],
            jnp.zeros((5, PIXC), F32),
        ],
        axis=0,
    )
    stats[0] = exact(table_rows, lambda v: dot_t(v, shell_pick))
    stat_copies = []
    for i in range(1, n):
        copy = remote(
            stats.at[0], stats.at[i], tsend.at[i], trecv.at[i], lax.rem(me + i, n)
        )
        copy.start()
        stat_copies.append(copy)
    kept = final[half]
    for copy in swaps:
        copy.wait_recv()
    swapped[half] = kept
    ready = []
    for h in range(2):
        bin_sums = swapped[h, DATA_TILES]
        ready.append(1.0 + exact(bin_sums, lambda v: dot(v, tables[2])))
    for copy in stat_copies:
        copy.wait_recv()
    sums = stats[0]
    for i in range(1, n):
        sums = sums + stats[i]
    fsc = sums[0:1] / jnp.sqrt(sums[1:2] * sums[2:3] + 1e-06)
    factor = jnp.broadcast_to((1.0 + fsc) / 2.0, (8, LANES))
    factor = exact(factor, lambda v: dot(v, shell_pick))[0:1, :]
    for h in range(2):
        scale = factor / ready[h]
        for t in range(DATA_TILES):
            lanes = slice(t * LANES, (t + 1) * LANES)
            k = t % (PIXC // LANES)
            value = swapped[h, t] * scale[:, k * LANES : (k + 1) * LANES]
            maps[0, h * rows : (h + 1) * rows, lanes] = value[:rows]

    for copy in line_copies[1:] + plane_copies + stat_copies:
        copy.wait_send()
    for copy in pair_sends + swaps:
        copy.wait_send()
    for group in plane_sends + class_sends + class_copies:
        for copy in group:
            copy.wait_send()


def write_out(maps, evidence, maps_out, evidence_out):
    maps_out[...] = maps[...]
    evidence_out[...] = evidence[...]


def solution(mesh):
    n = mesh.shape["ptcl"]
    ncls = mesh.shape["cls"]
    plane = 4
    line = n // plane
    rows = ORIENT // n
    pad = max(8, rows)
    block = 2 * pad
    own_rows = line * block
    nchunks = len(CHUNKS)

    def on_device(particles, panels, sigma2, defocus_bins, half_sets, prior_mask, orient_ids):
        count = particles.shape[0]
        dims = (n, ncls, plane, line, rows, pad, count)
        vmem = pl.BlockSpec(memory_space=pltpu.VMEM)
        hbm = pl.BlockSpec(memory_space=pltpu.HBM)
        dma = pltpu.SemaphoreType.DMA
        maps, evidence = pl.pallas_call(
            functools.partial(kernel, dims),
            out_shape=(
                jax.ShapeDtypeStruct((1, 2 * rows, 2 * PIXC), F32),
                jax.ShapeDtypeStruct((1, count), F32),
            ),
            in_specs=[hbm] + [vmem] * 7,
            out_specs=(vmem, vmem),
            scratch_shapes=[
                pltpu.VMEM((count, 2 * PIXC), BF16),
                pltpu.VMEM((count, 2 * PIXC), BF16),
                pltpu.VMEM((count, 2 * PIXC), BF16),
                pltpu.VMEM((n * block, PIXC), BF16),
                pltpu.VMEM((LANES, count), BF16),
                pltpu.VMEM((3, LANES, PIXC), BF16),
                pltpu.VMEM((8, PIXC), F32),
                pltpu.VMEM((ncls, HALVES, 2, count // HALVES), F32),
                pltpu.VMEM((n * block, count), F32),
                pltpu.VMEM((n * block, count), BF16),
                pltpu.VMEM((plane - 1, TILES, own_rows, LANES), BF16),
                pltpu.VMEM((plane - 1, TILES, own_rows, LANES), BF16),
                pltpu.VMEM((line, TILES, block, LANES), F32),
                pltpu.VMEM((line // 2, TILES, block, LANES), F32),
                pltpu.VMEM((line // 2 - 1, TILES, block, LANES), F32),
                pltpu.VMEM((2, TILES, pad, LANES), F32),
                pltpu.VMEM((2, TILES, pad, LANES), F32),
                pltpu.VMEM((8, WIDTH), F32),
                pltpu.VMEM((n, 8, LANES), F32),
                dma((4,)),
                dma((line, plane)),
                dma((line, plane)),
                dma((HALVES, ncls)),
                dma((HALVES, ncls)),
                dma((nchunks, plane)),
                dma((nchunks, plane)),
                dma((nchunks, line)),
                dma((nchunks, line)),
                dma((nchunks,)),
                dma((nchunks,)),
                dma((n,)),
                dma((n,)),
            ],
            compiler_params=pltpu.CompilerParams(
                collective_id=0, has_side_effects=True, vmem_limit_bytes=58 * 2**20
            ),
        )(
            particles,
            panels,
            sigma2.reshape(1, NSHELL),
            defocus_bins.reshape(1, count),
            half_sets.reshape(1, count),
            prior_mask.reshape(1, count),
            orient_ids.reshape(1, ORIENT),
            jnp.asarray(ctf_table()),
        )
        maps, evidence = pl.pallas_call(
            write_out,
            out_shape=(
                jax.ShapeDtypeStruct(maps.shape, F32),
                jax.ShapeDtypeStruct(evidence.shape, F32),
            ),
            in_specs=[vmem, vmem],
            out_specs=(vmem, vmem),
        )(maps, evidence)
        return maps, evidence.reshape(count)

    return jax.shard_map(
        on_device,
        mesh=mesh,
        in_specs=(
            P("ptcl", None),
            P("cls", "ptcl", None),
            P(),
            P("ptcl"),
            P("ptcl"),
            P("ptcl", "cls"),
            P(),
        ),
        out_specs=(P("cls", "ptcl", None), P("ptcl")),
        check_vma=False,
    )
```

```python
import functools

import jax
import jax.numpy as jnp
import numpy as np
from jax import lax
from jax.experimental import pallas as pl
from jax.experimental.pallas import tpu as pltpu
from jax.sharding import PartitionSpec as P

PIXC = 1024
ORIENT = 128
NSHELL = 32
NBIN = 16
LANES = 128
WIDTH = 2 * PIXC + LANES
TILES = WIDTH // LANES
DATA_TILES = TILES - 1
CHUNKS = ((12, 5), (0, 4), (4, 4), (8, 4))
KPARTS = 2
KWIDTH = PIXC // KPARTS
HALVES = 2
MESH = pl.DeviceIdType.MESH
BF16 = jnp.bfloat16
F32 = jnp.float32


def ctf_table():
    defocus = (np.arange(NBIN, dtype=np.float32) + np.float32(1.0)) / np.float32(NBIN)
    radius = (np.arange(PIXC, dtype=np.float32) + np.float32(0.5)) / np.float32(PIXC)
    phase = np.float32(0.3) + np.float32(2.5) * defocus[:, None] * radius[None, :]
    wide = phase.astype(np.float64)
    return (np.sin(wide) + 0.1 * np.cos(wide)).astype(np.float32)


def iota(shape, dim):
    return lax.broadcasted_iota(jnp.int32, shape, dim)


def over(values, size):
    return lax.shift_right_logical(values, jnp.int32(size.bit_length() - 1))


def mod(values, size):
    return lax.bitwise_and(values, jnp.int32(size - 1))


def dot(left, right):
    return lax.dot_general(left, right, (((1,), (0,)), ((), ())), preferred_element_type=F32)


def dot_t(left, right):
    return lax.dot_general(left, right, (((1,), (1,)), ((), ())), preferred_element_type=F32)


def split3(values):
    high = values.astype(BF16)
    rest = values - high.astype(F32)
    mid = rest.astype(BF16)
    low = (rest - mid.astype(F32)).astype(BF16)
    return high, mid, low


def exact(values, product):
    high, mid, low = split3(values)
    return product(high) + product(mid) + product(low)


def by_group(values, dim):
    high, mid, low = split3(values)
    axis = [1, 1]
    axis[dim] = values.shape[dim]
    group = over(iota(tuple(axis), dim), NBIN)
    mixed = jnp.where(
        group == 0,
        high.astype(F32),
        jnp.where(group == 1, mid.astype(F32), jnp.where(group == 2, low.astype(F32), 0.0)),
    )
    return mixed.astype(BF16)


def kernel(
    dims,
    particles,
    panels,
    sigma2,
    bins,
    halves,
    prior,
    orient,
    table,
    maps,
    evidence,
    images,
    weighted,
    centred,
    gathered,
    onehot,
    tables,
    noise,
    peaks,
    raw,
    posts,
    send1,
    recv1,
    acc,
    recv2,
    final,
    swapped,
    shells,
    stats,
    load_sem,
    gsend,
    grecv,
    csend,
    crecv,
    s1send,
    s1recv,
    s2send,
    s2recv,
    xsend,
    xrecv,
    tsend,
    trecv,
):
    n, ncls, plane, line, rows, pad, count = dims
    block = 2 * pad
    total_rows = n * block
    own_rows = line * block
    me = lax.axis_index("ptcl")
    mine = lax.axis_index("cls")
    q = lax.rem(me, plane)
    l = me // plane
    half = me // (n // 2)

    def at(line_pos, plane_pos):
        return line_pos * plane + plane_pos

    def remote(src, dst, send, recv, ptcl=None, cls=None):
        return pltpu.make_async_remote_copy(
            src_ref=src,
            dst_ref=dst,
            send_sem=send,
            recv_sem=recv,
            device_id=(mine if cls is None else cls, me if ptcl is None else ptcl),
            device_id_type=MESH,
        )

    barrier = pltpu.get_barrier_semaphore()
    for i in range(1, n):
        pl.semaphore_signal(
            barrier, inc=1, device_id=(mine, lax.rem(me + i, n)), device_id_type=MESH
        )
    for i in range(1, ncls):
        pl.semaphore_signal(
            barrier, inc=1, device_id=(lax.rem(mine + i, ncls), me), device_id_type=MESH
        )
    quarter = count // 4
    loads = []
    for i in range(4):
        span = pl.ds(i * quarter, quarter)
        loads.append(
            pltpu.make_async_copy(particles.at[span], images.at[span], load_sem.at[i])
        )
        loads[-1].start()

    piece = panels[0].astype(F32)
    real, imag = piece[:, :PIXC], piece[:, PIXC:]
    if rows < pad:
        fill = jnp.zeros((pad - rows, PIXC), F32)
        parts = [real, fill, imag, fill]
    else:
        parts = [real, imag]

    def spot(device, part):
        return gathered.at[part, pl.ds(pl.multiple_of(device * block, block), block)]

    staged = jnp.concatenate(parts, axis=0).astype(BF16)
    for part in range(KPARTS):
        gathered[part, pl.ds(pl.multiple_of(me * block, block), block), :] = staged[
            :, part * KWIDTH : (part + 1) * KWIDTH
        ]
    pl.semaphore_wait(barrier, n - 1 + ncls - 1)

    line_copies = [[None] for _ in range(KPARTS)]
    plane_copies = [[] for _ in range(KPARTS)]

    def forward(i, part):
        source = at(lax.rem(l + line - i, line), q)
        for p in range(1, plane):
            copy = remote(
                spot(source, part),
                spot(source, part),
                gsend.at[part, i, p],
                grecv.at[part, i, p],
                at(l, lax.rem(q + p, plane)),
            )
            copy.start()
            plane_copies[part].append(copy)

    for part in range(KPARTS):
        for i in range(1, line):
            copy = remote(
                spot(me, part),
                spot(me, part),
                gsend.at[part, i, 0],
                grecv.at[part, i, 0],
                at(lax.rem(l + i, line), q),
            )
            copy.start()
            line_copies[part].append(copy)
        forward(0, part)

    shell_pick = (iota((LANES, 1), 0) == over(iota((1, PIXC), 1), PIXC // NSHELL)).astype(
        F32
    ).astype(BF16)
    inverse = jnp.broadcast_to(1.0 / sigma2[...], (8, NSHELL))
    noise[...] = exact(inverse, lambda v: dot(v, shell_pick[:NSHELL]))
    base = table[...]
    base = jnp.concatenate(
        [base, base, base, jnp.zeros((LANES - 3 * NBIN, PIXC), F32)], axis=0
    )
    tables[0] = by_group(base, 0)
    tables[1] = (base * base * noise[0:1, :]).astype(BF16)
    tables[2] = (base * base).astype(BF16)
    row = iota((LANES, 1), 0)
    row = jnp.where(row < 3 * NBIN, mod(row, NBIN), -1)
    onehot[...] = (
        jnp.where(row == bins[...], 1.0, 0.0)
    ).astype(BF16)

    step = LANES

    def prepare(first, last):
        def body(i, carry):
            span = pl.ds(pl.multiple_of(i * step, step), step)
            picks = onehot[:, span]
            contrast = lax.dot_general(
                picks, tables[0], (((0,), (0,)), ((), ())), preferred_element_type=F32
            )
            level = noise[0:1, :]
            for part in range(2):
                cols = slice(part * PIXC, (part + 1) * PIXC)
                product = images[span, cols].astype(F32) * contrast
                centred[span, cols] = product.astype(BF16)
                weighted[span, cols] = (product * level).astype(BF16)
            return carry

        lax.fori_loop(first, last, body, 0)

    per = quarter // step
    for i in range(4):
        loads[i].wait()
        if i in (1, 2):
            for s in range(1, line):
                line_copies[i - 1][s].wait_recv()
                forward(s, i - 1)
        prepare(i * per, (i + 1) * per)

    ids = jnp.broadcast_to(orient[...].astype(F32), (8, ORIENT)).astype(BF16)
    c = iota((1, total_rows), 1)
    c_slot = mod(c, pad)
    c_part = mod(over(c, pad), 2)
    source_id = jnp.where(c_slot < rows, over(c, block) * rows + c_slot, -1)
    expand = jnp.where(source_id == iota((ORIENT, 1), 0), 1.0, 0.0).astype(BF16)
    ids_cols = dot(ids, expand)[0:1, :]
    square = (total_rows, total_rows)
    r = iota((total_rows, 1), 0)
    slot = mod(r, pad)
    r_sub = mod(over(r, block), line)
    r_line = mod(r_sub + l, line)
    r_plane = mod(over(r, own_rows) + q, plane)
    owner = at(r_line, r_plane)
    pairs = n // 2
    direction = mod(owner, pairs) * (2 * rows) + over(owner, pairs) * rows + slot
    direction = jnp.where(slot < rows, direction, -1).astype(F32)
    c_ok = c_slot < rows
    real_ids = jnp.where(c_ok & (c_part == 0), ids_cols, -2.0)
    imag_ids = jnp.where(c_ok & (c_part == 1), ids_cols, -2.0)
    pick_real = jnp.where(jnp.broadcast_to(direction, square) == real_ids, 1.0, 0.0).astype(BF16)
    pick_imag = jnp.where(jnp.broadcast_to(direction, square) == imag_ids, 1.0, 0.0).astype(BF16)
    row_half = mod(over(r, pad), 2)

    norm = jnp.zeros((total_rows, LANES), F32)
    for part in range(KPARTS):
        for copy in plane_copies[part]:
            copy.wait_recv()
        whole = gathered[part]
        panel_real = dot(pick_real, whole)
        panel_imag = dot(pick_imag, whole)
        panel_power = (panel_real * panel_real + panel_imag * panel_imag).astype(BF16)
        reals = slice(part * KWIDTH, (part + 1) * KWIDTH)
        imags = slice(PIXC + part * KWIDTH, PIXC + (part + 1) * KWIDTH)
        norm = norm + dot_t(panel_power, tables[1, :, reals])
        panel_real = panel_real.astype(BF16)
        panel_imag = panel_imag.astype(BF16)
        if part < KPARTS - 1:
            partial = dot_t(panel_real, weighted[:, reals]) + dot_t(
                panel_imag, weighted[:, imags]
            )
            raw[...] = partial if part == 0 else raw[...] + partial
    norm = by_group(norm, 1)
    valid = slot < rows
    class_copies = []
    lanes_each = count // HALVES
    for g in range(HALVES):
        span = slice(g * lanes_each, (g + 1) * lanes_each)
        scores = (
            raw[:, span]
            + dot_t(panel_real, weighted[span, reals])
            + dot_t(panel_imag, weighted[span, imags])
            - 0.5 * dot(norm, onehot[:, span])
        )
        use = (prior[:, span] > 0) & (halves[:, span] == row_half) & valid
        masked = jnp.where(use, scores, -1e30)
        local_peak = jnp.max(masked, axis=0, keepdims=True)
        value = jnp.where(use, jnp.exp(masked - local_peak), 0.0)
        raw[:, span] = value
        peaks[0, g, 0:1, :] = local_peak
        peaks[0, g, 1:2, :] = jnp.sum(value, axis=0, keepdims=True)
        group = []
        for i in range(1, ncls):
            copy = remote(
                peaks.at[0, g],
                peaks.at[i, g],
                csend.at[g, i],
                crecv.at[g, i],
                cls=lax.rem(mine + i, ncls),
            )
            copy.start()
            group.append(copy)
        class_copies.append(group)
    for g in range(HALVES):
        span = slice(g * lanes_each, (g + 1) * lanes_each)
        for copy in class_copies[g]:
            copy.wait_recv()
        local_peak = peaks[0, g, 0:1, :]
        peak = local_peak
        for i in range(1, ncls):
            peak = jnp.maximum(peak, peaks[i, g, 0:1, :])
        total = jnp.zeros_like(peak)
        for i in range(ncls):
            total = total + peaks[i, g, 1:2, :] * jnp.exp(peaks[i, g, 0:1, :] - peak)
        posts[:, span] = (raw[:, span] * (jnp.exp(local_peak - peak) / total)).astype(BF16)
        evidence[:, span] = peak + jnp.log(total)

    plane_sends, line_sends, swaps = [], [], []

    def launch(k):
        first, tiles = CHUNKS[k]
        data_tiles = min(tiles, DATA_TILES - first)
        start = first * LANES
        part = dot(posts[...], centred[:, start : start + data_tiles * LANES])
        for t in range(data_tiles):
            lanes = slice(t * LANES, (t + 1) * LANES)
            for i in range(line):
                acc[i, first + t] = part[i * block : (i + 1) * block, lanes]
            for p in range(1, plane):
                send1[p - 1, first + t] = part[
                    p * own_rows : (p + 1) * own_rows, lanes
                ].astype(BF16)
        if data_tiles < tiles:
            sums = dot_t(posts[...], onehot[...])
            kept = jnp.where(iota((1, LANES), 1) < NBIN, sums[:own_rows], 0.0)
            for i in range(line):
                acc[i, DATA_TILES] = kept[i * block : (i + 1) * block]
            for p in range(1, plane):
                send1[p - 1, DATA_TILES] = by_group(sums[p * own_rows : (p + 1) * own_rows], 1)
        span = pl.ds(first, tiles)
        group = []
        for p in range(1, plane):
            copy = remote(
                send1.at[p - 1, span],
                recv1.at[p - 1, span],
                s1send.at[k, p],
                s1recv.at[k, p],
                at(l, lax.rem(q + p, plane)),
            )
            copy.start()
            group.append(copy)
        plane_sends.append(group)

    def plane_sum(k):
        first, tiles = CHUNKS[k]
        span = pl.ds(first, tiles)
        for copy in plane_sends[k]:
            copy.wait_recv()
        for t in range(first, first + tiles):
            value = recv1[0, t].astype(F32)
            for p in range(2, plane):
                value = value + recv1[p - 1, t].astype(F32)
            for i in range(line):
                acc[i, t] = acc[i, t] + value[i * block : (i + 1) * block]
        group = []
        for i in range(1, line):
            copy = remote(
                acc.at[i, span],
                recv2.at[i - 1, span],
                s2send.at[k, i],
                s2recv.at[k, i],
                at(lax.rem(l + i, line), q),
            )
            copy.start()
            group.append(copy)
        line_sends.append(group)

    def finish(k):
        first, tiles = CHUNKS[k]
        span = pl.ds(first, tiles)
        for copy in line_sends[k]:
            copy.wait_recv()
        for t in range(first, first + tiles):
            value = acc[0, t]
            for i in range(1, line):
                value = value + recv2[i - 1, t]
            zero, one = value[:pad], value[pad:]
            final[0, t] = zero
            final[1, t] = one
            lanes = slice(t * LANES, (t + 1) * LANES)
            for i, product in enumerate((zero * one, zero * zero, one * one)):
                shells[i : i + 1, lanes] = jnp.sum(product, axis=0, keepdims=True)
        copy = remote(
            final.at[1 - half, span],
            swapped.at[half, span],
            xsend.at[k],
            xrecv.at[k],
            lax.rem(me + n // 2, n),
        )
        copy.start()
        swaps.append(copy)

    count_chunks = len(CHUNKS)
    for k in range(count_chunks):
        launch(k)
    for k in range(count_chunks + 1):
        if k < count_chunks:
            plane_sum(k)
        if k >= 1:
            finish(k - 1)

    table_rows = jnp.concatenate(
        [
            shells[0:3, :PIXC] + shells[0:3, PIXC : 2 * PIXC],
            jnp.zeros((5, PIXC), F32),
        ],
        axis=0,
    )
    stats[0] = exact(table_rows, lambda v: dot_t(v, shell_pick))
    stat_copies = []
    for i in range(1, n):
        copy = remote(
            stats.at[0], stats.at[i], tsend.at[i], trecv.at[i], lax.rem(me + i, n)
        )
        copy.start()
        stat_copies.append(copy)
    kept = final[half]
    for copy in swaps:
        copy.wait_recv()
    swapped[half] = kept
    ready = []
    for h in range(2):
        bin_sums = swapped[h, DATA_TILES]
        ready.append(1.0 + exact(bin_sums, lambda v: dot(v, tables[2])))
    for copy in stat_copies:
        copy.wait_recv()
    sums = stats[0]
    for i in range(1, n):
        sums = sums + stats[i]
    fsc = sums[0:1] / jnp.sqrt(sums[1:2] * sums[2:3] + 1e-06)
    factor = jnp.broadcast_to((1.0 + fsc) / 2.0, (8, LANES))
    factor = exact(factor, lambda v: dot(v, shell_pick))[0:1, :]
    for h in range(2):
        scale = factor / ready[h]
        for t in range(DATA_TILES):
            lanes = slice(t * LANES, (t + 1) * LANES)
            k = t % (PIXC // LANES)
            value = swapped[h, t] * scale[:, k * LANES : (k + 1) * LANES]
            maps[0, h * rows : (h + 1) * rows, lanes] = value[:rows]

    for part in range(KPARTS):
        for copy in line_copies[part][1:] + plane_copies[part]:
            copy.wait_send()
    for copy in stat_copies:
        copy.wait_send()
    for copy in swaps:
        copy.wait_send()
    for group in plane_sends + line_sends + class_copies:
        for copy in group:
            copy.wait_send()


def write_out(maps, evidence, maps_out, evidence_out):
    maps_out[...] = maps[...]
    evidence_out[...] = evidence[...]


def solution(mesh):
    n = mesh.shape["ptcl"]
    ncls = mesh.shape["cls"]
    plane = 4
    line = n // plane
    rows = ORIENT // n
    pad = max(8, rows)
    block = 2 * pad
    own_rows = line * block
    nchunks = len(CHUNKS)

    def on_device(particles, panels, sigma2, defocus_bins, half_sets, prior_mask, orient_ids):
        count = particles.shape[0]
        dims = (n, ncls, plane, line, rows, pad, count)
        vmem = pl.BlockSpec(memory_space=pltpu.VMEM)
        hbm = pl.BlockSpec(memory_space=pltpu.HBM)
        dma = pltpu.SemaphoreType.DMA
        maps, evidence = pl.pallas_call(
            functools.partial(kernel, dims),
            out_shape=(
                jax.ShapeDtypeStruct((1, 2 * rows, 2 * PIXC), F32),
                jax.ShapeDtypeStruct((1, count), F32),
            ),
            in_specs=[hbm] + [vmem] * 7,
            out_specs=(vmem, vmem),
            scratch_shapes=[
                pltpu.VMEM((count, 2 * PIXC), BF16),
                pltpu.VMEM((count, 2 * PIXC), BF16),
                pltpu.VMEM((count, 2 * PIXC), BF16),
                pltpu.VMEM((KPARTS, n * block, KWIDTH), BF16),
                pltpu.VMEM((LANES, count), BF16),
                pltpu.VMEM((3, LANES, PIXC), BF16),
                pltpu.VMEM((8, PIXC), F32),
                pltpu.VMEM((ncls, HALVES, 2, count // HALVES), F32),
                pltpu.VMEM((n * block, count), F32),
                pltpu.VMEM((n * block, count), BF16),
                pltpu.VMEM((plane - 1, TILES, own_rows, LANES), BF16),
                pltpu.VMEM((plane - 1, TILES, own_rows, LANES), BF16),
                pltpu.VMEM((line, TILES, block, LANES), F32),
                pltpu.VMEM((line - 1, TILES, block, LANES), F32),
                pltpu.VMEM((2, TILES, pad, LANES), F32),
                pltpu.VMEM((2, TILES, pad, LANES), F32),
                pltpu.VMEM((8, WIDTH), F32),
                pltpu.VMEM((n, 8, LANES), F32),
                dma((4,)),
                dma((KPARTS, line, plane)),
                dma((KPARTS, line, plane)),
                dma((HALVES, ncls)),
                dma((HALVES, ncls)),
                dma((nchunks, plane)),
                dma((nchunks, plane)),
                dma((nchunks, line)),
                dma((nchunks, line)),
                dma((nchunks,)),
                dma((nchunks,)),
                dma((n,)),
                dma((n,)),
            ],
            compiler_params=pltpu.CompilerParams(
                collective_id=0, has_side_effects=True, vmem_limit_bytes=58 * 2**20
            ),
        )(
            particles,
            panels,
            sigma2.reshape(1, NSHELL),
            defocus_bins.reshape(1, count),
            half_sets.reshape(1, count),
            prior_mask.reshape(1, count),
            orient_ids.reshape(1, ORIENT),
            jnp.asarray(ctf_table()),
        )
        maps, evidence = pl.pallas_call(
            write_out,
            out_shape=(
                jax.ShapeDtypeStruct(maps.shape, F32),
                jax.ShapeDtypeStruct(evidence.shape, F32),
            ),
            in_specs=[vmem, vmem],
            out_specs=(vmem, vmem),
        )(maps, evidence)
        return maps, evidence.reshape(count)

    return jax.shard_map(
        on_device,
        mesh=mesh,
        in_specs=(
            P("ptcl", None),
            P("cls", "ptcl", None),
            P(),
            P("ptcl"),
            P("ptcl"),
            P("ptcl", "cls"),
            P(),
        ),
        out_specs=(P("cls", "ptcl", None), P("ptcl")),
        check_vma=False,
    )
```

```python
import functools

import jax
import jax.numpy as jnp
import numpy as np
from jax import lax
from jax.experimental import pallas as pl
from jax.experimental.pallas import tpu as pltpu
from jax.sharding import PartitionSpec as P

PIXC = 1024
ORIENT = 128
NSHELL = 32
NBIN = 16
LANES = 128
WIDTH = 2 * PIXC + LANES
TILES = WIDTH // LANES
DATA_TILES = TILES - 1
CHUNKS = ((12, 5), (0, 4), (4, 4), (8, 4))
KPARTS = 2
KWIDTH = PIXC // KPARTS
HALVES = 2
MESH = pl.DeviceIdType.MESH
BF16 = jnp.bfloat16
F32 = jnp.float32


def ctf_table():
    defocus = (np.arange(NBIN, dtype=np.float32) + np.float32(1.0)) / np.float32(NBIN)
    radius = (np.arange(PIXC, dtype=np.float32) + np.float32(0.5)) / np.float32(PIXC)
    phase = np.float32(0.3) + np.float32(2.5) * defocus[:, None] * radius[None, :]
    wide = phase.astype(np.float64)
    return (np.sin(wide) + 0.1 * np.cos(wide)).astype(np.float32)


def iota(shape, dim):
    return lax.broadcasted_iota(jnp.int32, shape, dim)


def over(values, size):
    return lax.shift_right_logical(values, jnp.int32(size.bit_length() - 1))


def mod(values, size):
    return lax.bitwise_and(values, jnp.int32(size - 1))


def dot(left, right):
    return lax.dot_general(left, right, (((1,), (0,)), ((), ())), preferred_element_type=F32)


def dot_t(left, right):
    return lax.dot_general(left, right, (((1,), (1,)), ((), ())), preferred_element_type=F32)


def split3(values):
    high = values.astype(BF16)
    rest = values - high.astype(F32)
    mid = rest.astype(BF16)
    low = (rest - mid.astype(F32)).astype(BF16)
    return high, mid, low


def exact(values, product):
    high, mid, low = split3(values)
    return product(high) + product(mid) + product(low)


def by_group(values, dim):
    high, mid, low = split3(values)
    axis = [1, 1]
    axis[dim] = values.shape[dim]
    group = over(iota(tuple(axis), dim), NBIN)
    mixed = jnp.where(
        group == 0,
        high.astype(F32),
        jnp.where(group == 1, mid.astype(F32), jnp.where(group == 2, low.astype(F32), 0.0)),
    )
    return mixed.astype(BF16)


def kernel(
    dims,
    particles,
    panels,
    sigma2,
    bins,
    halves,
    prior,
    orient,
    table,
    maps,
    evidence,
    images,
    weighted,
    centred,
    gathered,
    onehot,
    tables,
    noise,
    peaks,
    raw,
    posts,
    send1,
    recv1,
    held,
    acc,
    recv2,
    final,
    swapped,
    shells,
    stats,
    load_sem,
    gsend,
    grecv,
    csend,
    crecv,
    s1send,
    s1recv,
    s2send,
    s2recv,
    xsend,
    xrecv,
    tsend,
    trecv,
):
    n, ncls, plane, line, rows, pad, count = dims
    block = 2 * pad
    total_rows = n * block
    own_rows = line * block
    me = lax.axis_index("ptcl")
    mine = lax.axis_index("cls")
    q = lax.rem(me, plane)
    l = me // plane
    half = me // (n // 2)

    def at(line_pos, plane_pos):
        return line_pos * plane + plane_pos

    def remote(src, dst, send, recv, ptcl=None, cls=None):
        return pltpu.make_async_remote_copy(
            src_ref=src,
            dst_ref=dst,
            send_sem=send,
            recv_sem=recv,
            device_id=(mine if cls is None else cls, me if ptcl is None else ptcl),
            device_id_type=MESH,
        )

    barrier = pltpu.get_barrier_semaphore()
    for i in range(1, n):
        pl.semaphore_signal(
            barrier, inc=1, device_id=(mine, lax.rem(me + i, n)), device_id_type=MESH
        )
    for i in range(1, ncls):
        pl.semaphore_signal(
            barrier, inc=1, device_id=(lax.rem(mine + i, ncls), me), device_id_type=MESH
        )
    quarter = count // 4
    loads = []
    for i in range(4):
        span = pl.ds(i * quarter, quarter)
        loads.append(
            pltpu.make_async_copy(particles.at[span], images.at[span], load_sem.at[i])
        )
        loads[-1].start()

    piece = panels[0].astype(F32)
    real, imag = piece[:, :PIXC], piece[:, PIXC:]
    if rows < pad:
        fill = jnp.zeros((pad - rows, PIXC), F32)
        parts = [real, fill, imag, fill]
    else:
        parts = [real, imag]

    def spot(device, part):
        return gathered.at[part, pl.ds(pl.multiple_of(device * block, block), block)]

    staged = jnp.concatenate(parts, axis=0).astype(BF16)
    for part in range(KPARTS):
        gathered[part, pl.ds(pl.multiple_of(me * block, block), block), :] = staged[
            :, part * KWIDTH : (part + 1) * KWIDTH
        ]
    pl.semaphore_wait(barrier, n - 1 + ncls - 1)

    line_copies = [[None] for _ in range(KPARTS)]
    plane_copies = [[] for _ in range(KPARTS)]

    def forward(i, part):
        source = at(lax.rem(l + line - i, line), q)
        for p in range(1, plane):
            copy = remote(
                spot(source, part),
                spot(source, part),
                gsend.at[part, i, p],
                grecv.at[part, i, p],
                at(l, lax.rem(q + p, plane)),
            )
            copy.start()
            plane_copies[part].append(copy)

    for part in range(KPARTS):
        for i in range(1, line):
            copy = remote(
                spot(me, part),
                spot(me, part),
                gsend.at[part, i, 0],
                grecv.at[part, i, 0],
                at(lax.rem(l + i, line), q),
            )
            copy.start()
            line_copies[part].append(copy)
        forward(0, part)

    shell_pick = (iota((LANES, 1), 0) == over(iota((1, PIXC), 1), PIXC // NSHELL)).astype(
        F32
    ).astype(BF16)
    inverse = jnp.broadcast_to(1.0 / sigma2[...], (8, NSHELL))
    noise[...] = exact(inverse, lambda v: dot(v, shell_pick[:NSHELL]))
    base = table[...]
    base = jnp.concatenate(
        [base, base, base, jnp.zeros((LANES - 3 * NBIN, PIXC), F32)], axis=0
    )
    tables[0] = by_group(base, 0)
    tables[1] = (base * base * noise[0:1, :]).astype(BF16)
    tables[2] = (base * base).astype(BF16)
    row = iota((LANES, 1), 0)
    row = jnp.where(row < 3 * NBIN, mod(row, NBIN), -1)
    onehot[...] = (
        jnp.where(row == bins[...], 1.0, 0.0)
    ).astype(BF16)

    step = LANES

    def prepare(first, last):
        def body(i, carry):
            span = pl.ds(pl.multiple_of(i * step, step), step)
            picks = onehot[:, span]
            contrast = lax.dot_general(
                picks, tables[0], (((0,), (0,)), ((), ())), preferred_element_type=F32
            )
            level = noise[0:1, :]
            for part in range(2):
                cols = slice(part * PIXC, (part + 1) * PIXC)
                product = images[span, cols].astype(F32) * contrast
                centred[span, cols] = product.astype(BF16)
                weighted[span, cols] = (product * level).astype(BF16)
            return carry

        lax.fori_loop(first, last, body, 0)

    per = quarter // step
    for i in range(4):
        loads[i].wait()
        if i in (1, 2):
            for s in range(1, line):
                line_copies[i - 1][s].wait_recv()
                forward(s, i - 1)
        prepare(i * per, (i + 1) * per)

    ids = jnp.broadcast_to(orient[...].astype(F32), (8, ORIENT)).astype(BF16)
    c = iota((1, total_rows), 1)
    c_slot = mod(c, pad)
    c_part = mod(over(c, pad), 2)
    source_id = jnp.where(c_slot < rows, over(c, block) * rows + c_slot, -1)
    expand = jnp.where(source_id == iota((ORIENT, 1), 0), 1.0, 0.0).astype(BF16)
    ids_cols = dot(ids, expand)[0:1, :]
    square = (total_rows, total_rows)
    r = iota((total_rows, 1), 0)
    slot = mod(r, pad)
    r_sub = mod(over(r, block), line)
    r_line = mod(r_sub + l, line)
    r_plane = lax.bitwise_xor(over(r, own_rows), q)
    owner = at(r_line, r_plane)
    pairs = n // 2
    direction = mod(owner, pairs) * (2 * rows) + over(owner, pairs) * rows + slot
    direction = jnp.where(slot < rows, direction, -1).astype(F32)
    c_ok = c_slot < rows
    real_ids = jnp.where(c_ok & (c_part == 0), ids_cols, -2.0)
    imag_ids = jnp.where(c_ok & (c_part == 1), ids_cols, -2.0)
    pick_real = jnp.where(jnp.broadcast_to(direction, square) == real_ids, 1.0, 0.0).astype(BF16)
    pick_imag = jnp.where(jnp.broadcast_to(direction, square) == imag_ids, 1.0, 0.0).astype(BF16)
    row_half = mod(over(r, pad), 2)

    norm = jnp.zeros((total_rows, LANES), F32)
    for part in range(KPARTS):
        for copy in plane_copies[part]:
            copy.wait_recv()
        whole = gathered[part]
        panel_real = dot(pick_real, whole)
        panel_imag = dot(pick_imag, whole)
        panel_power = (panel_real * panel_real + panel_imag * panel_imag).astype(BF16)
        reals = slice(part * KWIDTH, (part + 1) * KWIDTH)
        imags = slice(PIXC + part * KWIDTH, PIXC + (part + 1) * KWIDTH)
        norm = norm + dot_t(panel_power, tables[1, :, reals])
        panel_real = panel_real.astype(BF16)
        panel_imag = panel_imag.astype(BF16)
        if part < KPARTS - 1:
            partial = dot_t(panel_real, weighted[:, reals]) + dot_t(
                panel_imag, weighted[:, imags]
            )
            raw[...] = partial if part == 0 else raw[...] + partial
    norm = by_group(norm, 1)
    valid = slot < rows
    class_copies = []
    lanes_each = count // HALVES
    for g in range(HALVES):
        span = slice(g * lanes_each, (g + 1) * lanes_each)
        scores = (
            raw[:, span]
            + dot_t(panel_real, weighted[span, reals])
            + dot_t(panel_imag, weighted[span, imags])
            - 0.5 * dot(norm, onehot[:, span])
        )
        use = (prior[:, span] > 0) & (halves[:, span] == row_half) & valid
        masked = jnp.where(use, scores, -1e30)
        local_peak = jnp.max(masked, axis=0, keepdims=True)
        value = jnp.where(use, jnp.exp(masked - local_peak), 0.0)
        raw[:, span] = value
        peaks[0, g, 0:1, :] = local_peak
        peaks[0, g, 1:2, :] = jnp.sum(value, axis=0, keepdims=True)
        group = []
        for i in range(1, ncls):
            copy = remote(
                peaks.at[0, g],
                peaks.at[i, g],
                csend.at[g, i],
                crecv.at[g, i],
                cls=lax.rem(mine + i, ncls),
            )
            copy.start()
            group.append(copy)
        class_copies.append(group)
    for g in range(HALVES):
        span = slice(g * lanes_each, (g + 1) * lanes_each)
        for copy in class_copies[g]:
            copy.wait_recv()
        local_peak = peaks[0, g, 0:1, :]
        peak = local_peak
        for i in range(1, ncls):
            peak = jnp.maximum(peak, peaks[i, g, 0:1, :])
        total = jnp.zeros_like(peak)
        for i in range(ncls):
            total = total + peaks[i, g, 1:2, :] * jnp.exp(peaks[i, g, 0:1, :] - peak)
        posts[:, span] = (raw[:, span] * (jnp.exp(local_peak - peak) / total)).astype(BF16)
        evidence[:, span] = peak + jnp.log(total)

    plane_sends, line_sends, swaps = [], [], []

    def ways(k):
        return (1, 2) if k % 2 == 0 else (2, 1)

    def across(b):
        return lax.rem(lax.rem(q, 2) + b % 2, 2) + 2 * lax.rem(q // 2 + b // 2, 2)

    def launch(k):
        first, tiles = CHUNKS[k]
        data_tiles = min(tiles, DATA_TILES - first)
        near, far = ways(k)
        start = first * LANES
        part = dot(posts[...], centred[:, start : start + data_tiles * LANES])
        for t in range(data_tiles):
            lanes = slice(t * LANES, (t + 1) * LANES)
            for i in range(line):
                acc[i, first + t] = part[i * block : (i + 1) * block, lanes]
            for p in (near, 3):
                send1[p - 1, first + t] = part[
                    p * own_rows : (p + 1) * own_rows, lanes
                ].astype(BF16)
            held[first + t] = part[far * own_rows : (far + 1) * own_rows, lanes]
        if data_tiles < tiles:
            sums = dot_t(posts[...], onehot[...])
            kept = jnp.where(iota((1, LANES), 1) < NBIN, sums, 0.0)
            held[DATA_TILES] = kept[far * own_rows : (far + 1) * own_rows]
            for i in range(line):
                acc[i, DATA_TILES] = kept[i * block : (i + 1) * block]
            for p in (near, 3):
                send1[p - 1, DATA_TILES] = by_group(sums[p * own_rows : (p + 1) * own_rows], 1)
        span = pl.ds(first, tiles)
        near, far = ways(k)
        group = []
        for b in (3, near):
            copy = remote(
                send1.at[b - 1, span],
                recv1.at[b - 1, span],
                s1send.at[k, b],
                s1recv.at[k, b],
                at(l, across(near)),
            )
            copy.start()
            group.append(copy)
        plane_sends.append(group)

    def relay(k):
        first, tiles = CHUNKS[k]
        span = pl.ds(first, tiles)
        near, far = ways(k)
        plane_sends[k][0].wait_recv()
        for t in range(first, first + tiles):
            send1[far - 1, t] = (held[t] + recv1[2, t].astype(F32)).astype(BF16)
        copy = remote(
            send1.at[far - 1, span],
            recv1.at[far - 1, span],
            s1send.at[k, far],
            s1recv.at[k, far],
            at(l, across(far)),
        )
        copy.start()
        plane_sends[k].append(copy)

    def plane_sum(k):
        first, tiles = CHUNKS[k]
        span = pl.ds(first, tiles)
        plane_sends[k][1].wait_recv()
        plane_sends[k][2].wait_recv()
        for t in range(first, first + tiles):
            value = recv1[0, t].astype(F32) + recv1[1, t].astype(F32)
            for i in range(line):
                acc[i, t] = acc[i, t] + value[i * block : (i + 1) * block]
        group = []
        for i in range(1, line):
            copy = remote(
                acc.at[i, span],
                recv2.at[i - 1, span],
                s2send.at[k, i],
                s2recv.at[k, i],
                at(lax.rem(l + i, line), q),
            )
            copy.start()
            group.append(copy)
        line_sends.append(group)

    def finish(k):
        first, tiles = CHUNKS[k]
        span = pl.ds(first, tiles)
        for copy in line_sends[k]:
            copy.wait_recv()
        for t in range(first, first + tiles):
            value = acc[0, t]
            for i in range(1, line):
                value = value + recv2[i - 1, t]
            zero, one = value[:pad], value[pad:]
            final[0, t] = zero
            final[1, t] = one
            lanes = slice(t * LANES, (t + 1) * LANES)
            for i, product in enumerate((zero * one, zero * zero, one * one)):
                shells[i : i + 1, lanes] = jnp.sum(product, axis=0, keepdims=True)
        copy = remote(
            final.at[1 - half, span],
            swapped.at[half, span],
            xsend.at[k],
            xrecv.at[k],
            lax.rem(me + n // 2, n),
        )
        copy.start()
        swaps.append(copy)

    count_chunks = len(CHUNKS)
    for k in range(count_chunks):
        launch(k)
    for k in range(count_chunks + 2):
        if k < count_chunks:
            relay(k)
        if 1 <= k <= count_chunks:
            plane_sum(k - 1)
        if k >= 2:
            finish(k - 2)

    table_rows = jnp.concatenate(
        [
            shells[0:3, :PIXC] + shells[0:3, PIXC : 2 * PIXC],
            jnp.zeros((5, PIXC), F32),
        ],
        axis=0,
    )
    stats[0] = exact(table_rows, lambda v: dot_t(v, shell_pick))
    stat_copies = []
    for i in range(1, n):
        copy = remote(
            stats.at[0], stats.at[i], tsend.at[i], trecv.at[i], lax.rem(me + i, n)
        )
        copy.start()
        stat_copies.append(copy)
    kept = final[half]
    for copy in swaps:
        copy.wait_recv()
    swapped[half] = kept
    ready = []
    for h in range(2):
        bin_sums = swapped[h, DATA_TILES]
        ready.append(1.0 + exact(bin_sums, lambda v: dot(v, tables[2])))
    for copy in stat_copies:
        copy.wait_recv()
    sums = stats[0]
    for i in range(1, n):
        sums = sums + stats[i]
    fsc = sums[0:1] / jnp.sqrt(sums[1:2] * sums[2:3] + 1e-06)
    factor = jnp.broadcast_to((1.0 + fsc) / 2.0, (8, LANES))
    factor = exact(factor, lambda v: dot(v, shell_pick))[0:1, :]
    for h in range(2):
        scale = factor / ready[h]
        for t in range(DATA_TILES):
            lanes = slice(t * LANES, (t + 1) * LANES)
            k = t % (PIXC // LANES)
            value = swapped[h, t] * scale[:, k * LANES : (k + 1) * LANES]
            maps[0, h * rows : (h + 1) * rows, lanes] = value[:rows]

    for part in range(KPARTS):
        for copy in line_copies[part][1:] + plane_copies[part]:
            copy.wait_send()
    for copy in stat_copies:
        copy.wait_send()
    for copy in swaps:
        copy.wait_send()
    for group in plane_sends + line_sends + class_copies:
        for copy in group:
            copy.wait_send()


def write_out(maps, evidence, maps_out, evidence_out):
    maps_out[...] = maps[...]
    evidence_out[...] = evidence[...]


def solution(mesh):
    n = mesh.shape["ptcl"]
    ncls = mesh.shape["cls"]
    plane = 4
    line = n // plane
    rows = ORIENT // n
    pad = max(8, rows)
    block = 2 * pad
    own_rows = line * block
    nchunks = len(CHUNKS)

    def on_device(particles, panels, sigma2, defocus_bins, half_sets, prior_mask, orient_ids):
        count = particles.shape[0]
        dims = (n, ncls, plane, line, rows, pad, count)
        vmem = pl.BlockSpec(memory_space=pltpu.VMEM)
        hbm = pl.BlockSpec(memory_space=pltpu.HBM)
        dma = pltpu.SemaphoreType.DMA
        maps, evidence = pl.pallas_call(
            functools.partial(kernel, dims),
            out_shape=(
                jax.ShapeDtypeStruct((1, 2 * rows, 2 * PIXC), F32),
                jax.ShapeDtypeStruct((1, count), F32),
            ),
            in_specs=[hbm] + [vmem] * 7,
            out_specs=(vmem, vmem),
            scratch_shapes=[
                pltpu.VMEM((count, 2 * PIXC), BF16),
                pltpu.VMEM((count, 2 * PIXC), BF16),
                pltpu.VMEM((count, 2 * PIXC), BF16),
                pltpu.VMEM((KPARTS, n * block, KWIDTH), BF16),
                pltpu.VMEM((LANES, count), BF16),
                pltpu.VMEM((3, LANES, PIXC), BF16),
                pltpu.VMEM((8, PIXC), F32),
                pltpu.VMEM((ncls, HALVES, 2, count // HALVES), F32),
                pltpu.VMEM((n * block, count), F32),
                pltpu.VMEM((n * block, count), BF16),
                pltpu.VMEM((plane - 1, TILES, own_rows, LANES), BF16),
                pltpu.VMEM((plane - 1, TILES, own_rows, LANES), BF16),
                pltpu.VMEM((TILES, own_rows, LANES), F32),
                pltpu.VMEM((line, TILES, block, LANES), F32),
                pltpu.VMEM((line - 1, TILES, block, LANES), F32),
                pltpu.VMEM((2, TILES, pad, LANES), F32),
                pltpu.VMEM((2, TILES, pad, LANES), F32),
                pltpu.VMEM((8, WIDTH), F32),
                pltpu.VMEM((n, 8, LANES), F32),
                dma((4,)),
                dma((KPARTS, line, plane)),
                dma((KPARTS, line, plane)),
                dma((HALVES, ncls)),
                dma((HALVES, ncls)),
                dma((nchunks, plane)),
                dma((nchunks, plane)),
                dma((nchunks, line)),
                dma((nchunks, line)),
                dma((nchunks,)),
                dma((nchunks,)),
                dma((n,)),
                dma((n,)),
            ],
            compiler_params=pltpu.CompilerParams(
                collective_id=0, has_side_effects=True, vmem_limit_bytes=58 * 2**20
            ),
        )(
            particles,
            panels,
            sigma2.reshape(1, NSHELL),
            defocus_bins.reshape(1, count),
            half_sets.reshape(1, count),
            prior_mask.reshape(1, count),
            orient_ids.reshape(1, ORIENT),
            jnp.asarray(ctf_table()),
        )
        maps, evidence = pl.pallas_call(
            write_out,
            out_shape=(
                jax.ShapeDtypeStruct(maps.shape, F32),
                jax.ShapeDtypeStruct(evidence.shape, F32),
            ),
            in_specs=[vmem, vmem],
            out_specs=(vmem, vmem),
        )(maps, evidence)
        return maps, evidence.reshape(count)

    return jax.shard_map(
        on_device,
        mesh=mesh,
        in_specs=(
            P("ptcl", None),
            P("cls", "ptcl", None),
            P(),
            P("ptcl"),
            P("ptcl"),
            P("ptcl", "cls"),
            P(),
        ),
        out_specs=(P("cls", "ptcl", None), P("ptcl")),
        check_vma=False,
    )
```

```python
import functools

import jax
import jax.numpy as jnp
import numpy as np
from jax import lax
from jax.experimental import pallas as pl
from jax.experimental.pallas import tpu as pltpu
from jax.sharding import PartitionSpec as P

PIXC = 1024
ORIENT = 128
NSHELL = 32
NBIN = 16
LANES = 128
WIDTH = 2 * PIXC + LANES
TILES = WIDTH // LANES
DATA_TILES = TILES - 1
CHUNKS = ((12, 5), (0, 4), (4, 4), (8, 4))
KPARTS = 2
KWIDTH = PIXC // KPARTS
HALVES = 2
MESH = pl.DeviceIdType.MESH
BF16 = jnp.bfloat16
F32 = jnp.float32


def ctf_table():
    defocus = (np.arange(NBIN, dtype=np.float32) + np.float32(1.0)) / np.float32(NBIN)
    radius = (np.arange(PIXC, dtype=np.float32) + np.float32(0.5)) / np.float32(PIXC)
    phase = np.float32(0.3) + np.float32(2.5) * defocus[:, None] * radius[None, :]
    wide = phase.astype(np.float64)
    return (np.sin(wide) + 0.1 * np.cos(wide)).astype(np.float32)


def iota(shape, dim):
    return lax.broadcasted_iota(jnp.int32, shape, dim)


def over(values, size):
    return lax.shift_right_logical(values, jnp.int32(size.bit_length() - 1))


def mod(values, size):
    return lax.bitwise_and(values, jnp.int32(size - 1))


def dot(left, right):
    return lax.dot_general(left, right, (((1,), (0,)), ((), ())), preferred_element_type=F32)


def dot_t(left, right):
    return lax.dot_general(left, right, (((1,), (1,)), ((), ())), preferred_element_type=F32)


def split3(values):
    high = values.astype(BF16)
    rest = values - high.astype(F32)
    mid = rest.astype(BF16)
    low = (rest - mid.astype(F32)).astype(BF16)
    return high, mid, low


def exact(values, product):
    high, mid, low = split3(values)
    return product(high) + product(mid) + product(low)


def by_group(values, dim):
    high, mid, low = split3(values)
    axis = [1, 1]
    axis[dim] = values.shape[dim]
    group = over(iota(tuple(axis), dim), NBIN)
    mixed = jnp.where(
        group == 0,
        high.astype(F32),
        jnp.where(group == 1, mid.astype(F32), jnp.where(group == 2, low.astype(F32), 0.0)),
    )
    return mixed.astype(BF16)


def kernel(
    dims,
    particles,
    panels,
    sigma2,
    bins,
    halves,
    prior,
    orient,
    table,
    maps,
    evidence,
    images,
    weighted,
    centred,
    gathered,
    onehot,
    tables,
    noise,
    peaks,
    raw,
    posts,
    send1,
    recv1,
    acc,
    recv2,
    final,
    swapped,
    shells,
    stats,
    load_sem,
    gsend,
    grecv,
    csend,
    crecv,
    s1send,
    s1recv,
    s2send,
    s2recv,
    xsend,
    xrecv,
    tsend,
    trecv,
):
    n, ncls, plane, line, rows, pad, count = dims
    block = 2 * pad
    total_rows = n * block
    own_rows = line * block
    me = lax.axis_index("ptcl")
    mine = lax.axis_index("cls")
    q = lax.rem(me, plane)
    l = me // plane
    half = me // (n // 2)

    def at(line_pos, plane_pos):
        return line_pos * plane + plane_pos

    def remote(src, dst, send, recv, ptcl=None, cls=None):
        return pltpu.make_async_remote_copy(
            src_ref=src,
            dst_ref=dst,
            send_sem=send,
            recv_sem=recv,
            device_id=(mine if cls is None else cls, me if ptcl is None else ptcl),
            device_id_type=MESH,
        )

    barrier = pltpu.get_barrier_semaphore()
    for i in range(1, n):
        pl.semaphore_signal(
            barrier, inc=1, device_id=(mine, lax.rem(me + i, n)), device_id_type=MESH
        )
    for i in range(1, ncls):
        pl.semaphore_signal(
            barrier, inc=1, device_id=(lax.rem(mine + i, ncls), me), device_id_type=MESH
        )
    quarter = count // 4
    loads = []
    for i in range(4):
        span = pl.ds(i * quarter, quarter)
        loads.append(
            pltpu.make_async_copy(particles.at[span], images.at[span], load_sem.at[i])
        )
        loads[-1].start()

    piece = panels[0].astype(F32)
    real, imag = piece[:, :PIXC], piece[:, PIXC:]
    if rows < pad:
        fill = jnp.zeros((pad - rows, PIXC), F32)
        parts = [real, fill, imag, fill]
    else:
        parts = [real, imag]

    def spot(device, part):
        return gathered.at[part, pl.ds(pl.multiple_of(device * block, block), block)]

    staged = jnp.concatenate(parts, axis=0).astype(BF16)
    for part in range(KPARTS):
        gathered[part, pl.ds(pl.multiple_of(me * block, block), block), :] = staged[
            :, part * KWIDTH : (part + 1) * KWIDTH
        ]
    pl.semaphore_wait(barrier, n - 1 + ncls - 1)

    panel_copies = [[] for _ in range(KPARTS)]
    for part in range(KPARTS):
        for i in reversed(range(line)):
            for p in range(plane):
                if i == 0 and p == 0:
                    continue
                copy = remote(
                    spot(me, part),
                    spot(me, part),
                    gsend.at[part, i, p],
                    grecv.at[part, i, p],
                    at(lax.rem(l + i, line), lax.rem(q + p, plane)),
                )
                copy.start()
                panel_copies[part].append(copy)

    shell_pick = (iota((LANES, 1), 0) == over(iota((1, PIXC), 1), PIXC // NSHELL)).astype(
        F32
    ).astype(BF16)
    inverse = jnp.broadcast_to(1.0 / sigma2[...], (8, NSHELL))
    noise[...] = exact(inverse, lambda v: dot(v, shell_pick[:NSHELL]))
    base = table[...]
    base = jnp.concatenate(
        [base, base, base, jnp.zeros((LANES - 3 * NBIN, PIXC), F32)], axis=0
    )
    tables[0] = by_group(base, 0)
    tables[1] = (base * base * noise[0:1, :]).astype(BF16)
    tables[2] = (base * base).astype(BF16)
    row = iota((LANES, 1), 0)
    row = jnp.where(row < 3 * NBIN, mod(row, NBIN), -1)
    onehot[...] = (
        jnp.where(row == bins[...], 1.0, 0.0)
    ).astype(BF16)

    step = LANES

    def prepare(first, last):
        def body(i, carry):
            span = pl.ds(pl.multiple_of(i * step, step), step)
            picks = onehot[:, span]
            contrast = lax.dot_general(
                picks, tables[0], (((0,), (0,)), ((), ())), preferred_element_type=F32
            )
            level = noise[0:1, :]
            for part in range(2):
                cols = slice(part * PIXC, (part + 1) * PIXC)
                product = images[span, cols].astype(F32) * contrast
                centred[span, cols] = product.astype(BF16)
                weighted[span, cols] = (product * level).astype(BF16)
            return carry

        lax.fori_loop(first, last, body, 0)

    per = quarter // step
    for i in range(4):
        loads[i].wait()
        prepare(i * per, (i + 1) * per)

    ids = jnp.broadcast_to(orient[...].astype(F32), (8, ORIENT)).astype(BF16)
    c = iota((1, total_rows), 1)
    c_slot = mod(c, pad)
    c_part = mod(over(c, pad), 2)
    source_id = jnp.where(c_slot < rows, over(c, block) * rows + c_slot, -1)
    expand = jnp.where(source_id == iota((ORIENT, 1), 0), 1.0, 0.0).astype(BF16)
    ids_cols = dot(ids, expand)[0:1, :]
    square = (total_rows, total_rows)
    r = iota((total_rows, 1), 0)
    slot = mod(r, pad)
    r_sub = mod(over(r, block), line)
    r_line = mod(r_sub + l, line)
    r_plane = mod(over(r, own_rows) + q, plane)
    owner = at(r_line, r_plane)
    pairs = n // 2
    direction = mod(owner, pairs) * (2 * rows) + over(owner, pairs) * rows + slot
    direction = jnp.where(slot < rows, direction, -1).astype(F32)
    c_ok = c_slot < rows
    real_ids = jnp.where(c_ok & (c_part == 0), ids_cols, -2.0)
    imag_ids = jnp.where(c_ok & (c_part == 1), ids_cols, -2.0)
    pick_real = jnp.where(jnp.broadcast_to(direction, square) == real_ids, 1.0, 0.0).astype(BF16)
    pick_imag = jnp.where(jnp.broadcast_to(direction, square) == imag_ids, 1.0, 0.0).astype(BF16)
    row_half = mod(over(r, pad), 2)

    norm = jnp.zeros((total_rows, LANES), F32)
    for part in range(KPARTS):
        for copy in panel_copies[part]:
            copy.wait_recv()
        whole = gathered[part]
        panel_real = dot(pick_real, whole)
        panel_imag = dot(pick_imag, whole)
        panel_power = (panel_real * panel_real + panel_imag * panel_imag).astype(BF16)
        reals = slice(part * KWIDTH, (part + 1) * KWIDTH)
        imags = slice(PIXC + part * KWIDTH, PIXC + (part + 1) * KWIDTH)
        norm = norm + dot_t(panel_power, tables[1, :, reals])
        panel_real = panel_real.astype(BF16)
        panel_imag = panel_imag.astype(BF16)
        if part < KPARTS - 1:
            partial = dot_t(panel_real, weighted[:, reals]) + dot_t(
                panel_imag, weighted[:, imags]
            )
            raw[...] = partial if part == 0 else raw[...] + partial
    norm = by_group(norm, 1)
    valid = slot < rows
    class_copies = []
    lanes_each = count // HALVES
    for g in range(HALVES):
        span = slice(g * lanes_each, (g + 1) * lanes_each)
        scores = (
            raw[:, span]
            + dot_t(panel_real, weighted[span, reals])
            + dot_t(panel_imag, weighted[span, imags])
            - 0.5 * dot(norm, onehot[:, span])
        )
        use = (prior[:, span] > 0) & (halves[:, span] == row_half) & valid
        masked = jnp.where(use, scores, -1e30)
        local_peak = jnp.max(masked, axis=0, keepdims=True)
        value = jnp.where(use, jnp.exp(masked - local_peak), 0.0)
        raw[:, span] = value
        peaks[0, g, 0:1, :] = local_peak
        peaks[0, g, 1:2, :] = jnp.sum(value, axis=0, keepdims=True)
        group = []
        for i in range(1, ncls):
            copy = remote(
                peaks.at[0, g],
                peaks.at[i, g],
                csend.at[g, i],
                crecv.at[g, i],
                cls=lax.rem(mine + i, ncls),
            )
            copy.start()
            group.append(copy)
        class_copies.append(group)
    for g in range(HALVES):
        span = slice(g * lanes_each, (g + 1) * lanes_each)
        for copy in class_copies[g]:
            copy.wait_recv()
        local_peak = peaks[0, g, 0:1, :]
        peak = local_peak
        for i in range(1, ncls):
            peak = jnp.maximum(peak, peaks[i, g, 0:1, :])
        total = jnp.zeros_like(peak)
        for i in range(ncls):
            total = total + peaks[i, g, 1:2, :] * jnp.exp(peaks[i, g, 0:1, :] - peak)
        posts[:, span] = (raw[:, span] * (jnp.exp(local_peak - peak) / total)).astype(BF16)
        evidence[:, span] = peak + jnp.log(total)

    plane_sends, line_sends, swaps = [], [], []

    def launch(k):
        first, tiles = CHUNKS[k]
        data_tiles = min(tiles, DATA_TILES - first)
        start = first * LANES
        part = dot(posts[...], centred[:, start : start + data_tiles * LANES])
        for t in range(data_tiles):
            lanes = slice(t * LANES, (t + 1) * LANES)
            for i in range(line):
                acc[i, first + t] = part[i * block : (i + 1) * block, lanes]
            for p in range(1, plane):
                send1[p - 1, first + t] = part[
                    p * own_rows : (p + 1) * own_rows, lanes
                ].astype(BF16)
        if data_tiles < tiles:
            sums = dot_t(posts[...], onehot[...])
            kept = jnp.where(iota((1, LANES), 1) < NBIN, sums[:own_rows], 0.0)
            for i in range(line):
                acc[i, DATA_TILES] = kept[i * block : (i + 1) * block]
            for p in range(1, plane):
                send1[p - 1, DATA_TILES] = by_group(sums[p * own_rows : (p + 1) * own_rows], 1)
        span = pl.ds(first, tiles)
        group = []
        for p in range(1, plane):
            copy = remote(
                send1.at[p - 1, span],
                recv1.at[p - 1, span],
                s1send.at[k, p],
                s1recv.at[k, p],
                at(l, lax.rem(q + p, plane)),
            )
            copy.start()
            group.append(copy)
        plane_sends.append(group)

    def plane_sum(k):
        first, tiles = CHUNKS[k]
        span = pl.ds(first, tiles)
        for copy in plane_sends[k]:
            copy.wait_recv()
        for t in range(first, first + tiles):
            value = recv1[0, t].astype(F32)
            for p in range(2, plane):
                value = value + recv1[p - 1, t].astype(F32)
            for i in range(line):
                acc[i, t] = acc[i, t] + value[i * block : (i + 1) * block]
        group = []
        for i in range(1, line):
            copy = remote(
                acc.at[i, span],
                recv2.at[i - 1, span],
                s2send.at[k, i],
                s2recv.at[k, i],
                at(lax.rem(l + i, line), q),
            )
            copy.start()
            group.append(copy)
        line_sends.append(group)

    def finish(k):
        first, tiles = CHUNKS[k]
        span = pl.ds(first, tiles)
        for copy in line_sends[k]:
            copy.wait_recv()
        for t in range(first, first + tiles):
            value = acc[0, t]
            for i in range(1, line):
                value = value + recv2[i - 1, t]
            zero, one = value[:pad], value[pad:]
            final[0, t] = zero
            final[1, t] = one
            lanes = slice(t * LANES, (t + 1) * LANES)
            for i, product in enumerate((zero * one, zero * zero, one * one)):
                shells[i : i + 1, lanes] = jnp.sum(product, axis=0, keepdims=True)
        copy = remote(
            final.at[1 - half, span],
            swapped.at[half, span],
            xsend.at[k],
            xrecv.at[k],
            lax.rem(me + n // 2, n),
        )
        copy.start()
        swaps.append(copy)

    count_chunks = len(CHUNKS)
    for k in range(count_chunks):
        launch(k)
    for k in range(count_chunks + 1):
        if k < count_chunks:
            plane_sum(k)
        if k >= 1:
            finish(k - 1)

    table_rows = jnp.concatenate(
        [
            shells[0:3, :PIXC] + shells[0:3, PIXC : 2 * PIXC],
            jnp.zeros((5, PIXC), F32),
        ],
        axis=0,
    )
    stats[0] = exact(table_rows, lambda v: dot_t(v, shell_pick))
    stat_copies = []
    for i in range(1, n):
        copy = remote(
            stats.at[0], stats.at[i], tsend.at[i], trecv.at[i], lax.rem(me + i, n)
        )
        copy.start()
        stat_copies.append(copy)
    kept = final[half]
    for copy in swaps:
        copy.wait_recv()
    swapped[half] = kept
    ready = []
    for h in range(2):
        bin_sums = swapped[h, DATA_TILES]
        ready.append(1.0 + exact(bin_sums, lambda v: dot(v, tables[2])))
    for copy in stat_copies:
        copy.wait_recv()
    sums = stats[0]
    for i in range(1, n):
        sums = sums + stats[i]
    fsc = sums[0:1] / jnp.sqrt(sums[1:2] * sums[2:3] + 1e-06)
    factor = jnp.broadcast_to((1.0 + fsc) / 2.0, (8, LANES))
    factor = exact(factor, lambda v: dot(v, shell_pick))[0:1, :]
    for h in range(2):
        scale = factor / ready[h]
        for t in range(DATA_TILES):
            lanes = slice(t * LANES, (t + 1) * LANES)
            k = t % (PIXC // LANES)
            value = swapped[h, t] * scale[:, k * LANES : (k + 1) * LANES]
            maps[0, h * rows : (h + 1) * rows, lanes] = value[:rows]

    for part in range(KPARTS):
        for copy in panel_copies[part]:
            copy.wait_send()
    for copy in stat_copies:
        copy.wait_send()
    for copy in swaps:
        copy.wait_send()
    for group in plane_sends + line_sends + class_copies:
        for copy in group:
            copy.wait_send()


def write_out(maps, evidence, maps_out, evidence_out):
    maps_out[...] = maps[...]
    evidence_out[...] = evidence[...]


def solution(mesh):
    n = mesh.shape["ptcl"]
    ncls = mesh.shape["cls"]
    plane = 4
    line = n // plane
    rows = ORIENT // n
    pad = max(8, rows)
    block = 2 * pad
    own_rows = line * block
    nchunks = len(CHUNKS)

    def on_device(particles, panels, sigma2, defocus_bins, half_sets, prior_mask, orient_ids):
        count = particles.shape[0]
        dims = (n, ncls, plane, line, rows, pad, count)
        vmem = pl.BlockSpec(memory_space=pltpu.VMEM)
        hbm = pl.BlockSpec(memory_space=pltpu.HBM)
        dma = pltpu.SemaphoreType.DMA
        maps, evidence = pl.pallas_call(
            functools.partial(kernel, dims),
            out_shape=(
                jax.ShapeDtypeStruct((1, 2 * rows, 2 * PIXC), F32),
                jax.ShapeDtypeStruct((1, count), F32),
            ),
            in_specs=[hbm] + [vmem] * 7,
            out_specs=(vmem, vmem),
            scratch_shapes=[
                pltpu.VMEM((count, 2 * PIXC), BF16),
                pltpu.VMEM((count, 2 * PIXC), BF16),
                pltpu.VMEM((count, 2 * PIXC), BF16),
                pltpu.VMEM((KPARTS, n * block, KWIDTH), BF16),
                pltpu.VMEM((LANES, count), BF16),
                pltpu.VMEM((3, LANES, PIXC), BF16),
                pltpu.VMEM((8, PIXC), F32),
                pltpu.VMEM((ncls, HALVES, 2, count // HALVES), F32),
                pltpu.VMEM((n * block, count), F32),
                pltpu.VMEM((n * block, count), BF16),
                pltpu.VMEM((plane - 1, TILES, own_rows, LANES), BF16),
                pltpu.VMEM((plane - 1, TILES, own_rows, LANES), BF16),
                pltpu.VMEM((line, TILES, block, LANES), F32),
                pltpu.VMEM((line - 1, TILES, block, LANES), F32),
                pltpu.VMEM((2, TILES, pad, LANES), F32),
                pltpu.VMEM((2, TILES, pad, LANES), F32),
                pltpu.VMEM((8, WIDTH), F32),
                pltpu.VMEM((n, 8, LANES), F32),
                dma((4,)),
                dma((KPARTS, line, plane)),
                dma((KPARTS, line, plane)),
                dma((HALVES, ncls)),
                dma((HALVES, ncls)),
                dma((nchunks, plane)),
                dma((nchunks, plane)),
                dma((nchunks, line)),
                dma((nchunks, line)),
                dma((nchunks,)),
                dma((nchunks,)),
                dma((n,)),
                dma((n,)),
            ],
            compiler_params=pltpu.CompilerParams(
                collective_id=0, has_side_effects=True, vmem_limit_bytes=58 * 2**20
            ),
        )(
            particles,
            panels,
            sigma2.reshape(1, NSHELL),
            defocus_bins.reshape(1, count),
            half_sets.reshape(1, count),
            prior_mask.reshape(1, count),
            orient_ids.reshape(1, ORIENT),
            jnp.asarray(ctf_table()),
        )
        maps, evidence = pl.pallas_call(
            write_out,
            out_shape=(
                jax.ShapeDtypeStruct(maps.shape, F32),
                jax.ShapeDtypeStruct(evidence.shape, F32),
            ),
            in_specs=[vmem, vmem],
            out_specs=(vmem, vmem),
        )(maps, evidence)
        return maps, evidence.reshape(count)

    return jax.shard_map(
        on_device,
        mesh=mesh,
        in_specs=(
            P("ptcl", None),
            P("cls", "ptcl", None),
            P(),
            P("ptcl"),
            P("ptcl"),
            P("ptcl", "cls"),
            P(),
        ),
        out_specs=(P("cls", "ptcl", None), P("ptcl")),
        check_vma=False,
    )
```
